128 devices in a mesh: dp: 4 (over x), seq: 32 (over z, y, core).
Axes of the slice: x: 4, y: 4, z: 4, core: 2. Of those that a mesh axis runs over, the one named last changes fastest.
Arguments:
- tile_feats: bfloat16 [65536, 1536], P(('dp', 'seq')), may hold values from -6 to 6, as said below
- tile_dest: int32 [65536, 1], P(('dp', 'seq')), may hold values from 0 to 127; in each aligned block of 512 rows (0 to 511, 512 to 1023, ...) at most 8 rows name the same one
- embed_weight: bfloat16 [1536, 768], replicated, may hold values from -0.15625 to 0.15625
- norm1_gain: float32 [768], replicated, may hold values from 0.1 to 1.9
- qkv_weight: bfloat16 [768, 2304], replicated, may hold values from -0.21875 to 0.21875
- out_weight: bfloat16 [768, 768], replicated, may hold values from -0.21875 to 0.21875
- norm2_gain: float32 [768], replicated, may hold values from 0.1 to 1.9
- up_weight: bfloat16 [768, 3072], replicated, may hold values from -0.21875 to 0.21875
- down_weight: bfloat16 [3072, 768], replicated, may hold values from -0.109375 to 0.109375
Outputs:
- tile_out: bfloat16 [65536, 768], P(('dp', 'seq'))
- far_heads: float32 [4, 16, 512, 48], P('dp', None, 'seq')
The draws below stay inside these ranges and needn't reach their ends.
Inputs may be any that keep to these rules, and one draw needn't show every extreme that they name: `tile_dest`: destination devices are numbered over dp then seq. Among the 512 tiles of one device at most 8 name the same destination, and some device reaches 8; every device is named by some tile. `tile_feats`: some tiles' embeddings are entirely zero; they are real tiles like any other.
All inputs are finite; a program needn't handle non-finite values.
Results may differ from the reference program's by a relative error of at most 0.012.
Values may be sent and summed in bfloat16 or wider, within the bound.
A program may use at most 128 MiB of HBM per device.

```python
import math
import jax
import jax.numpy as jnp
import numpy as np
from jax import lax

F = 1536
D = 768
HEADS = 16
FF = 3072
HEAD_DIM = 48
RATE = 64
TILE_DEV = 512
CAP = 8
SLOTS = 1024
SEQ_LEN = 32768
TILES = 65536
N_DP = 4
N_SEQ = 32
DEVICES = 128


def draw_tile_feats(key, part):
    key = jax.random.fold_in(key, 11)
    value_key, row_key = jax.random.split(key, 2)
    blank = jax.random.randint(row_key, (TILES, 1), 0, 4) == 0
    values = jax.random.truncated_normal(value_key, -6.0, 6.0, (TILES, F), jnp.float32)
    return jnp.where(blank, 0.0, values).astype(jnp.bfloat16)


def assign_block(stream_key, own, number, rows, amount, top, limit, slope):
    ranking = jax.random.permutation(stream_key, amount)
    packed, ordinary = shares(amount, rows * top, limit, slope, True), shares(amount, rows * top, limit, slope, False)
    places = jnp.arange(amount)

    def named(lengths, offset_by):
        used = int((lengths > 0).sum())
        fixed = max(1, used // 4)
        passed = fixed + (places - fixed + offset_by * (used - fixed)) % max(1, amount - fixed)
        return jnp.zeros((amount,), jnp.int32).at[ranking[jnp.where(places < fixed, places, passed)]].set(jnp.asarray(lengths, jnp.int32))

    lengths = jnp.where(number % 4 == 0, named(packed, number // 4), named(ordinary, number - number // 4 - 1))
    mixed = jax.random.permutation(jax.random.fold_in(own, 3), amount)
    source_of, taker = mixed[0:amount // 2 * 2:2], mixed[1:amount // 2 * 2:2]
    margin = jnp.minimum(lengths[source_of] - 1, limit - lengths[taker]) // 2
    margin = jnp.where((source_of == ranking[0]) | (taker == ranking[0]) | (lengths[taker] == 0), 0, jnp.maximum(margin, 0))
    passed = jax.random.randint(jax.random.fold_in(own, 4), (amount // 2,), 0, 1 << 20) % (margin + 1)
    lengths = lengths.at[source_of].add(-passed).at[taker].add(passed)
    members = jnp.searchsorted(jnp.cumsum(lengths), jnp.arange(rows * top), side="right").astype(jnp.int32)
    grid = members.reshape(top, rows).T
    grid = grid[jax.random.permutation(jax.random.fold_in(own, 1), rows)]
    offset_by = jax.random.randint(jax.random.fold_in(own, 2), (rows, 1), 0, top)
    return jnp.take_along_axis(grid, (jnp.arange(top)[None, :] + offset_by) % top, axis=1)


def shares(amount, total, limit, skew, full):
    weights = [(1 << 20) // math.isqrt(rank ** skew) + 1 for rank in range(1, amount + 1)]
    largest = limit if full else min(limit, max(-(-total // amount), total * weights[0] // sum(weights)))
    least = 1 if total - largest >= amount - 1 else 0
    counts, rest = [largest] + [least] * (amount - 1), total - largest - least * (amount - 1)
    while rest > 0:
        movable = [i for i in range(1, amount) if counts[i] < largest] or [i for i in range(1, amount) if counts[i] < limit]
        pool, remaining = sum([weights[i] for i in movable]), rest
        for i in movable:
            addition = min(limit - counts[i], max(1, remaining * weights[i] // pool), rest)
            counts[i] = counts[i] + addition
            rest = rest - addition
    return np.array(counts)


def noise(rng, extent, scale, most, held_as=jnp.bfloat16):
    return jnp.clip(scale * jax.random.normal(rng, extent, jnp.float32), -most, most).astype(held_as)


def setup_inputs(seed: int = 0) -> dict:
    streams_of = jax.random.split(jax.random.key(seed), 10)
    tile_feats = draw_tile_feats(jax.random.fold_in(streams_of[9], 71), 0)
    tile_dest_keys = jax.random.split(jax.random.fold_in(streams_of[1], 1), TILES // TILE_DEV)
    tile_dest_turns = jax.random.permutation(jax.random.fold_in(streams_of[1], 3), TILES // TILE_DEV)
    tile_dest = jax.vmap(lambda own, number: assign_block(jax.random.fold_in(streams_of[1], 2), own, number, TILE_DEV, DEVICES, 1, CAP, 2))(tile_dest_keys, tile_dest_turns).reshape((TILES, 1))
    embed_weight = noise(streams_of[2], (F, D), F ** -0.5, 0.15625)
    norm1_gain = jnp.clip(1.0 + 0.18 * jax.random.normal(streams_of[3], (D,), jnp.float32), 0.1, 1.9)
    qkv_weight = noise(streams_of[4], (D, 3 * D), D ** -0.5, 0.21875)
    out_weight = noise(streams_of[5], (D, D), D ** -0.5, 0.21875)
    norm2_gain = jnp.clip(1.0 + 0.18 * jax.random.normal(streams_of[6], (D,), jnp.float32), 0.1, 1.9)
    up_weight = noise(streams_of[7], (D, FF), D ** -0.5, 0.21875)
    down_weight = noise(streams_of[8], (FF, D), FF ** -0.5, 0.109375)
    return dict(tile_feats=tile_feats, tile_dest=tile_dest, embed_weight=embed_weight, norm1_gain=norm1_gain, qkv_weight=qkv_weight, out_weight=out_weight, norm2_gain=norm2_gain, up_weight=up_weight, down_weight=down_weight)


epsilon = 1e-05
masked = -1e+30

def layer_norm(activations, norm_gain):
    widened = activations.astype(jnp.float32)
    row_mean = lax.optimization_barrier(jnp.mean(widened, axis=-1, keepdims=True))
    centred = widened - row_mean
    spread = lax.optimization_barrier(jnp.mean(centred * centred, axis=-1, keepdims=True))
    return (centred * lax.rsqrt(spread + epsilon) * norm_gain).astype(jnp.bfloat16)

def feed_forward(activations, norm_gain, up_weight, down_weight):
    normed = layer_norm(activations, norm_gain)
    inner_act = jax.nn.gelu(jnp.dot(normed, up_weight, preferred_element_type=jnp.float32)).astype(jnp.bfloat16)
    summed = activations.astype(jnp.float32) + jnp.dot(inner_act, down_weight, preferred_element_type=jnp.float32)
    return summed.astype(jnp.bfloat16)

def attend(queries, key_rows, value_rows, key_valid):
    score_scale = queries.shape[-1] ** (-0.5)
    scores = jnp.einsum('qd,kd->qk', queries.astype(jnp.float32), key_rows.astype(jnp.float32)) * score_scale
    scores = jnp.where(key_valid[None, :], scores, masked)
    row_max = lax.optimization_barrier(jnp.max(scores, axis=-1, keepdims=True))
    exponent = jnp.exp(scores - row_max)
    row_sum = lax.optimization_barrier(jnp.sum(exponent, axis=-1, keepdims=True))
    weights = (exponent / row_sum).astype(jnp.bfloat16)
    result = jnp.einsum('qk,kd->qd', weights.astype(jnp.float32), value_rows.astype(jnp.float32))
    return (result, row_max[:, 0] + jnp.log(row_sum[:, 0]))

def blend_branches(near_out, near_lse, far_out, far_lse):
    larger = jnp.maximum(near_lse, far_lse)
    near_weight = jnp.exp(near_lse - larger)
    far_weight = jnp.exp(far_lse - larger)
    return (near_weight[..., None] * near_out + far_weight[..., None] * far_out) / (near_weight + far_weight)[..., None]

def encode(sequence, valid_rows, norm1_gain, qkv_weight, out_weight, norm2_gain, up_weight, down_weight):
    length = sequence.shape[0]
    blocks = length // SLOTS
    strided = length // RATE
    normed = layer_norm(sequence, norm1_gain)
    projected = jnp.dot(normed, qkv_weight, preferred_element_type=jnp.float32).astype(jnp.bfloat16)
    projected = projected.reshape(length, 3, HEADS, HEAD_DIM)
    queries = jnp.transpose(projected[:, 0], (1, 0, 2))
    key_rows = jnp.transpose(projected[:, 1], (1, 0, 2))
    value_rows = jnp.transpose(projected[:, 2], (1, 0, 2))

    def to_blocks(stacked):
        return jnp.transpose(stacked.reshape(HEADS, blocks, SLOTS, HEAD_DIM), (1, 0, 2, 3))

    def local_block(operands):
        return jax.vmap(attend, in_axes=(0, 0, 0, None))(operands[0], operands[1], operands[2], operands[3])
    near_out, near_lse = lax.map(local_block, (to_blocks(queries), to_blocks(key_rows), to_blocks(value_rows), valid_rows.reshape(blocks, SLOTS)))
    near_out = jnp.transpose(near_out, (1, 0, 2, 3)).reshape(HEADS, strided, RATE, HEAD_DIM)
    near_lse = jnp.transpose(near_lse, (1, 0, 2)).reshape(HEADS, strided, RATE)
    chosen = jnp.arange(HEADS)

    def select_rows(stacked):
        return stacked.reshape(HEADS, strided, RATE, HEAD_DIM)[chosen, :, chosen]
    far_valid = valid_rows.reshape(strided, RATE)[:, :HEADS].T
    far_out, far_lse = jax.vmap(attend)(select_rows(queries), select_rows(key_rows), select_rows(value_rows), far_valid)
    joined = blend_branches(near_out, near_lse, far_out[:, :, None, :], far_lse[:, :, None])
    dilated = (jnp.arange(RATE)[None, :] == chosen[:, None])[:, None, :, None]
    mixed_heads = jnp.where(dilated, joined, near_out)
    mixed_heads = jnp.transpose(mixed_heads.reshape(HEADS, length, HEAD_DIM), (1, 0, 2)).reshape(length, D).astype(jnp.bfloat16)
    hidden_state = (sequence.astype(jnp.float32) + jnp.dot(mixed_heads, out_weight, preferred_element_type=jnp.float32)).astype(jnp.bfloat16)
    return (feed_forward(hidden_state, norm2_gain, up_weight, down_weight), far_out.astype(jnp.float32))

def reference(tile_feats, tile_dest, embed_weight, norm1_gain, qkv_weight, out_weight, norm2_gain, up_weight, down_weight):
    embedded = jnp.dot(tile_feats, embed_weight, preferred_element_type=jnp.float32).astype(jnp.bfloat16)
    destination = tile_dest[:, 0].astype(jnp.int32)
    by_device = destination.reshape(DEVICES, TILE_DEV)
    onehot = (by_device[:, :, None] == jnp.arange(DEVICES, dtype=jnp.int32)[None, None, :]).astype(jnp.int32)
    rank_in = (lax.optimization_barrier(jnp.sum(jnp.cumsum(onehot, axis=1) * onehot, axis=2)) - 1).reshape(TILES).astype(jnp.int32)
    source = (jnp.arange(TILES, dtype=jnp.int32) // TILE_DEV).astype(jnp.int32)
    group_index = (destination // N_SEQ).astype(jnp.int32)
    position = (destination % N_SEQ * SLOTS + source * CAP + rank_in).astype(jnp.int32)
    sequences = jnp.zeros((N_DP, SEQ_LEN, D), jnp.bfloat16).at[group_index, position].set(embedded)
    valid_flags = jnp.zeros((N_DP, SEQ_LEN), jnp.int32).at[group_index, position].set(1)

    def one_group(operands):
        return encode(operands[0], operands[1] > 0, norm1_gain, qkv_weight, out_weight, norm2_gain, up_weight, down_weight)
    outputs, far_heads = lax.map(one_group, (sequences, valid_flags))
    return (outputs[group_index, position], far_heads)
```

```python
import functools
import math

import jax
import jax.numpy as jnp
from jax import lax
from jax.experimental import pallas as pl
from jax.experimental.pallas import tpu as pltpu
from jax.sharding import PartitionSpec as P

F32 = jnp.float32
BF16 = jnp.bfloat16
MESH = pl.DeviceIdType.MESH
HEADS = 16
HEAD = 48
D = 768
F = 1536
FF = 3072
TILES = 512
SLOTS = 1024
CAP = 8
N_DP = 4
N_SEQ = 32
DEVICES = 128
RATE = 64
ROWS = SLOTS // RATE
QUERIES = 512
FF_BLOCK = 512
EPSILON = 1e-5
MASKED = -1e30
EMPTY = 1e30
SCALE = HEAD ** -0.5 * math.log2(math.e)
NT = (((1,), (1,)), ((), ()))
TN = (((0,), (0,)), ((), ()))


def dot(a, b):
    return jnp.dot(a, b, preferred_element_type=F32)


def iota(shape, axis):
    return lax.broadcasted_iota(jnp.int32, shape, axis)


def layer_norm(x, gain):
    centred = x - jnp.mean(x, axis=1, keepdims=True)
    spread = jnp.mean(centred * centred, axis=1, keepdims=True)
    return (centred * lax.rsqrt(spread + EPSILON) * gain).astype(BF16)


def to_message(rows):
    n, w = rows.shape
    left = rows[:, : w // 2].reshape(n // CAP, CAP, w // 2)
    right = rows[:, w // 2 :].reshape(n // CAP, CAP, w // 2)
    return jnp.concatenate([left, right], axis=1).astype(BF16)


def from_message(message):
    n, _, w = message.shape
    wide = message.astype(F32)
    left = wide[:, :CAP].reshape(n * CAP, w)
    right = wide[:, CAP:].reshape(n * CAP, w)
    return jnp.concatenate([left, right], axis=1)


def kernel(
    feats_hbm, dest_ref, embed_hbm, gain1_ref, qkv_hbm, out_hbm, gain2_ref, up_hbm, down_hbm,
    tile_ref, far_ref,
    feats, embed_w, qkv_w, out_w, up_w, down_w, qkv_t,
    embedded, normed, slot_col, send1, recv1, x_ref, bias_ref,
    q_t, k_ref, v_t, scores, near, peak, mixed,
    far_send, far_recv, res_send, res_recv, far_t,
    send2, recv2, hidden, total,
    load_sem, send1_sem, recv1_sem, fsend_sem, frecv_sem, rsend_sem, rrecv_sem, send2_sem, recv2_sem,
):
    dp, sq = lax.axis_index("dp"), lax.axis_index("seq")
    me = dp * N_SEQ + sq

    def partner(k):
        k = (k * 37) % DEVICES
        x = (dp + k // 32) % 4
        z = (sq // 8 + (k // 8) % 4) % 4
        y = (sq // 2 + (k // 2) % 4) % 4
        return x, z * 8 + y * 2 + (sq + k) % 2

    loads = [
        pltpu.make_async_copy(src, dst, load_sem.at[i])
        for i, (src, dst) in enumerate(
            [(feats_hbm, feats), (embed_hbm, embed_w), (qkv_hbm, qkv_w), (out_hbm, out_w), (up_hbm, up_w), (down_hbm, down_w)]
        )
    ]
    for load in loads:
        load.start()

    barrier = pltpu.get_barrier_semaphore()

    def greet(k, carry):
        x, s = partner(k)
        pl.semaphore_signal(barrier, inc=1, device_id=(x, s), device_id_type=MESH)
        return carry

    lax.fori_loop(1, DEVICES, greet, 0)

    dest = dest_ref[...]
    onehot = (dest == iota((TILES, DEVICES), 1)).astype(F32)
    below = (iota((TILES, TILES), 1) < iota((TILES, TILES), 0)).astype(BF16)
    rank = jnp.sum(dot(below, onehot.astype(BF16)) * onehot, axis=1, keepdims=True)
    slots = dest.astype(F32) * CAP + rank
    slot_col[...] = jnp.broadcast_to(slots, (TILES, 128))
    slot_row = jnp.transpose(slot_col[...])[0:1, :].astype(jnp.int32)

    loads[0].wait()
    loads[1].wait()
    for i in range(4):
        rows = pl.ds(i * 128, 128)
        tile_rows = dot(feats[rows, :], embed_w[...]).astype(BF16)
        embedded[rows, :] = tile_rows
        normed[rows, :] = layer_norm(tile_rows.astype(F32), gain1_ref[...])

    def pack(i, carry):
        place = (iota((256, TILES), 0) + i * 256 == slot_row).astype(F32)
        rows = dot(place.astype(BF16), normed[...])
        used = jnp.sum(place, axis=1, keepdims=True)
        first = jnp.where((iota((256, 128), 1) == 0) & (used < 0.5), EMPTY, rows[:, :128])
        send1[pl.ds(i * 32, 32)] = to_message(jnp.concatenate([first, rows[:, 128:]], axis=1))
        return carry

    lax.fori_loop(0, 4, pack, 0)
    pl.semaphore_wait(barrier, DEVICES - 1)

    def send_rows(k, carry):
        x, s = partner(k)
        pltpu.make_async_remote_copy(
            src_ref=send1.at[x * N_SEQ + s], dst_ref=recv1.at[me], send_sem=send1_sem, recv_sem=recv1_sem.at[me],
            device_id=(x, s), device_id_type=MESH,
        ).start()
        return carry

    lax.fori_loop(1, DEVICES, send_rows, 0)
    pltpu.make_async_copy(send1.at[me], recv1.at[me], recv1_sem.at[me]).start()

    loads[2].wait()

    def turn(i, carry):
        columns = pl.ds(pl.multiple_of(i * 128, 128), 128)
        qkv_t[columns, :] = jnp.transpose(qkv_w[:, columns].astype(F32)).astype(BF16)
        return carry

    lax.fori_loop(0, 3 * D // 128, turn, 0)
    one_row = (iota((16, SLOTS), 0) == 0).astype(BF16)
    for h in range(HEADS):
        base = 64 * (h % 2)
        q_t[h, pl.ds(64 - base, 64), :] = jnp.zeros((64, SLOTS), BF16)
        q_t[h, pl.ds(base + HEAD, 16), :] = one_row
        v_t[h, pl.ds(HEAD, 16), :] = jnp.ones((16, SLOTS), BF16)

    def arrived1(s, carry):
        pltpu.make_async_copy(send1.at[s], recv1.at[s], recv1_sem.at[s]).wait()
        return carry

    lax.fori_loop(0, DEVICES, arrived1, 0)

    def project(g, carry):
        rows = from_message(recv1[pl.ds(g * 32, 32)])
        empty = rows[:, 0:1] > 0.1 * EMPTY
        rows = jnp.where(empty, 0.0, rows).astype(BF16)
        bias = jnp.broadcast_to(jnp.where(empty, MASKED, 0.0), (256, 128))
        x_ref[pl.ds(g * 4, 4)] = rows.reshape(4, RATE, D)
        bias_ref[pl.ds(g * 4, 4)] = bias.astype(BF16).reshape(4, RATE, 128)
        lanes = pl.ds(pl.multiple_of(g * 256, 256), 256)
        query = (lax.dot_general(qkv_t[0:D, :], rows, NT, preferred_element_type=F32) * SCALE).astype(BF16)
        for h in range(HEADS):
            q_t[h, pl.ds(64 * (h % 2), HEAD), lanes] = query[h * HEAD : (h + 1) * HEAD]
        key = lax.dot_general(qkv_t[D : 2 * D, :], rows, NT, preferred_element_type=F32)
        masks = jnp.where(iota((16, 256), 0) == 0, jnp.transpose(bias)[0:16, :], 0.0)
        for p in range(HEADS // 2):
            pair = jnp.concatenate(
                [key[96 * p : 96 * p + 48], masks, key[96 * p + 48 : 96 * p + 96], masks], axis=0
            )
            k_ref[p, pl.ds(pl.multiple_of(g * 256, 256), 256), :] = jnp.transpose(pair).astype(BF16)
        value = lax.dot_general(qkv_t[2 * D :, :], rows, NT, preferred_element_type=F32).astype(BF16)
        for h in range(HEADS):
            v_t[h, pl.ds(0, HEAD), lanes] = value[h * HEAD : (h + 1) * HEAD]
        return carry

    lax.fori_loop(0, 4, project, 0)

    rows = x_ref[:, pl.ds(0, 16), :].reshape(256, D)
    swap = (iota((256, 256), 1) == (iota((256, 256), 0) & 15) * 16 + (iota((256, 256), 0) >> 4)).astype(BF16)
    rows = dot(swap, rows).astype(BF16)
    bias = dot(swap, bias_ref[:, pl.ds(0, 16), :].reshape(256, 128))
    low = HEAD * (iota((256, D), 0) >> 4)
    column = iota((256, D), 1)
    own = (column >= low) & (column < low + HEAD)
    turns = (iota((D, 128), 0) - iota((D, 128), 1)).astype(F32) * (1.0 / HEAD)
    whole = jnp.abs(turns - jnp.round(turns)) < 0.01
    lane = iota((D, 128), 1)
    to_front = (whole & (lane < HEAD)).astype(BF16)
    turns = turns + (64.0 / HEAD)
    whole = jnp.abs(turns - jnp.round(turns)) < 0.01
    to_back = (whole & (lane >= 64) & (lane < 64 + HEAD)).astype(BF16)

    def own_head(part, scale):
        product = dot(rows, qkv_w[:, part * D : (part + 1) * D]) * scale
        return jnp.where(own, product, 0.0).astype(BF16)

    lane = iota((256, 128), 1)
    far_q = jnp.where(lane == HEAD, 1.0, dot(own_head(0, SCALE), to_front))
    far_kv = dot(own_head(1, 1.0), to_front) + dot(own_head(2, 1.0), to_back)
    far_kv = jnp.where(lane == HEAD, bias, jnp.where(lane == 64 + HEAD, 1.0, far_kv))
    far_send[...] = jnp.concatenate(
        [far_q.reshape(HEADS, ROWS, 128), far_kv.reshape(HEADS, ROWS, 128)], axis=1
    ).astype(BF16)

    def send_far(h, carry):
        @pl.when(2 * h != sq)
        def _():
            pltpu.make_async_remote_copy(
                src_ref=far_send.at[h], dst_ref=far_recv.at[sq], send_sem=fsend_sem, recv_sem=frecv_sem.at[sq],
                device_id=(dp, 2 * h), device_id_type=MESH,
            ).start()

        @pl.when(2 * h == sq)
        def _():
            pltpu.make_async_copy(far_send.at[h], far_recv.at[sq], frecv_sem.at[sq]).start()

        return carry

    lax.fori_loop(0, HEADS, send_far, 0)

    parts = SLOTS // QUERIES

    def score(h, i):
        return lax.dot_general(
            k_ref[h // 2], q_t[h, :, i * QUERIES : (i + 1) * QUERIES], (((1,), (0,)), ((), ())), preferred_element_type=F32
        )

    def attend(first, last):
        scores[0] = score(first, 0)

        def one_head(h, carry):
            for i in range(parts):
                if i + 1 < parts:
                    later = score(h, i + 1)
                else:
                    later = score(jnp.minimum(h + 1, last - 1), 0)
                block = scores[i % 2]
                top = jnp.max(block, axis=0, keepdims=True)
                weights = jnp.exp2(block - top).astype(BF16)
                near[h, :, i * QUERIES : (i + 1) * QUERIES] = dot(v_t[h], weights)
                peak[h, :, i * QUERIES : (i + 1) * QUERIES] = jnp.broadcast_to(top, (8, QUERIES))
                scores[(i + 1) % 2] = later
            return carry

        lax.fori_loop(first, last, one_head, 0)

    def far_branch():
        def arrived(s, carry):
            pltpu.make_async_copy(far_recv.at[s], far_recv.at[s], frecv_sem.at[s]).wait()
            return carry

        lax.fori_loop(0, N_SEQ, arrived, 0)
        queries = far_recv[:, pl.ds(0, 16), :].reshape(N_SEQ * ROWS, 128)
        pairs = far_recv[:, pl.ds(16, 16), :].reshape(N_SEQ * ROWS, 128)
        block = lax.dot_general(queries, pairs, NT, preferred_element_type=F32)
        top = jnp.max(block, axis=1, keepdims=True)
        result = dot(jnp.exp2(block - top).astype(BF16), pairs)
        summed = result[:, 64 + HEAD : 65 + HEAD]
        result = jnp.where(iota(result.shape, 1) < 64, top + jnp.log2(summed), result / summed)
        res_send[...] = result.reshape(N_SEQ, ROWS, 128)
        head = sq // 2

        def answer(s, carry):
            @pl.when(s != sq)
            def _():
                pltpu.make_async_remote_copy(
                    src_ref=res_send.at[s], dst_ref=res_recv.at[head], send_sem=rsend_sem, recv_sem=rrecv_sem.at[head],
                    device_id=(dp, s), device_id_type=MESH,
                ).start()

            return carry

        lax.fori_loop(0, N_SEQ, answer, 0)
        pltpu.make_async_copy(res_send.at[sq], res_recv.at[head], rrecv_sem.at[head]).start()
        pltpu.make_async_copy(
            res_send.at[pl.ds(0, N_SEQ - 1)], res_send.at[pl.ds(0, N_SEQ - 1)], rsend_sem
        ).wait()

    def far_arrived():
        def arrived(h, carry):
            pltpu.make_async_copy(res_recv.at[h], res_recv.at[h], rrecv_sem.at[h]).wait()
            return carry

        lax.fori_loop(0, HEADS, arrived, 0)
        results = res_recv[...].reshape(HEADS * ROWS, 128)
        far_ref[...] = res_recv[:, :, 64 : 64 + HEAD]
        lane = iota((HEADS * ROWS, 128), 1)
        high = results.astype(BF16).astype(F32)
        middle = (results - high).astype(BF16).astype(F32)
        lowest = results - high - middle
        split = jnp.where(lane >= 64, results, jnp.where(lane == 0, high, jnp.where(lane == 1, middle, lowest)))
        row = iota((HEADS * ROWS, SLOTS), 0)
        spread = (iota((HEADS * ROWS, SLOTS), 1) == (row & 15) * RATE + (row >> 4)).astype(BF16)
        far_t[...] = lax.dot_general(split.astype(BF16), spread, TN, preferred_element_type=F32)

    def blend(first, last):
        def one_head(h, carry):
            summed = near[h, HEAD : HEAD + 1, :]
            near_lse = peak[h, 0:1, :] + jnp.log2(summed)
            far_lse = far_t[0:1, :] + far_t[1:2, :] + far_t[2:3, :]
            far_lse = jnp.where((iota((1, SLOTS), 1) & (RATE - 1)) == h, far_lse, MASKED)
            larger = jnp.maximum(near_lse, far_lse)
            near_weight = jnp.exp2(near_lse - larger)
            far_weight = jnp.exp2(far_lse - larger)
            both = near_weight + far_weight
            joined = near[h, 0:HEAD, :] * (near_weight / (both * summed)) + far_t[64 : 64 + HEAD, :] * (far_weight / both)
            mixed[pl.ds(pl.multiple_of(h * HEAD, 16), HEAD), :] = joined.astype(BF16)
            return carry

        lax.fori_loop(first, last, one_head, 0)

    def give_back(c):
        def pack_back(g, carry):
            lanes = pl.ds(pl.multiple_of(g * 256, 256), 256)
            rows = jnp.transpose(mixed[256 * c : 256 * (c + 1), lanes].astype(F32))
            send2[c, pl.ds(g * 32, 32)] = to_message(rows)
            return carry

        lax.fori_loop(0, 4, pack_back, 0)

        def send_back(k, carry):
            x, s = partner(k)
            pltpu.make_async_remote_copy(
                src_ref=send2.at[c, x * N_SEQ + s], dst_ref=recv2.at[c, me], send_sem=send2_sem.at[c], recv_sem=recv2_sem.at[c, me],
                device_id=(x, s), device_id_type=MESH,
            ).start()
            return carry

        lax.fori_loop(1, DEVICES, send_back, 0)
        pltpu.make_async_copy(send2.at[c, me], recv2.at[c, me], recv2_sem.at[c, me]).start()

    attend(0, 3)

    @pl.when(sq % 2 == 0)
    def _():
        far_branch()

    attend(3, 6)
    far_arrived()
    blend(0, 6)
    give_back(0)
    attend(6, 11)
    blend(6, 11)
    give_back(1)
    attend(11, 16)
    blend(11, 16)
    give_back(2)

    loads[3].wait()
    hidden[...] = embedded[...].astype(F32)
    for c in range(3):
        def arrived2(s, carry, c=c):
            pltpu.make_async_copy(send2.at[c, s], recv2.at[c, s], recv2_sem.at[c, s]).wait()
            return carry

        lax.fori_loop(0, DEVICES, arrived2, 0)
        taken = jnp.zeros((TILES, 256), F32)
        for g in range(4):
            place = (iota((TILES, 256), 1) + g * 256 == slot_col[:, 0:1].astype(jnp.int32)).astype(BF16)
            taken = taken + dot(place, from_message(recv2[c, pl.ds(g * 32, 32)]).astype(BF16))
        hidden[...] += dot(taken.astype(BF16), out_w[256 * c : 256 * (c + 1), :])
    loads[4].wait()
    loads[5].wait()
    state = hidden[...].astype(BF16).astype(F32)
    normed[...] = layer_norm(state, gain2_ref[...])
    total[...] = state

    def feed(i, carry):
        columns = pl.ds(pl.multiple_of(i * FF_BLOCK, FF_BLOCK), FF_BLOCK)
        inner = dot(normed[...], up_w[:, columns])
        inner = jax.nn.gelu(inner, approximate=True).astype(BF16)
        total[...] += dot(inner, down_w[columns, :])
        return carry

    lax.fori_loop(0, FF // FF_BLOCK, feed, 0)
    tile_ref[...] = total[...].astype(BF16)

    most = pl.ds(0, DEVICES - 1)
    pltpu.make_async_copy(send1.at[most], send1.at[most], send1_sem).wait()
    for c in range(3):
        pltpu.make_async_copy(send2.at[c, most], send2.at[c, most], send2_sem.at[c]).wait()

    @pl.when(sq % 2 == 0)
    def _():
        pltpu.make_async_copy(far_send.at[pl.ds(0, 15)], far_send.at[pl.ds(0, 15)], fsend_sem).wait()

    @pl.when(sq % 2 == 1)
    def _():
        pltpu.make_async_copy(far_send, far_send, fsend_sem).wait()


def on_device(tile_feats, tile_dest, embed_weight, norm1_gain, qkv_weight, out_weight, norm2_gain, up_weight, down_weight):
    hbm = pl.BlockSpec(memory_space=pl.ANY)
    vmem = pl.BlockSpec(memory_space=pltpu.VMEM)
    dma = pltpu.SemaphoreType.DMA
    tile_out, far_heads = pl.pallas_call(
        kernel,
        out_shape=(
            jax.ShapeDtypeStruct((TILES, D), BF16),
            jax.ShapeDtypeStruct((HEADS, ROWS, HEAD), F32),
        ),
        in_specs=[hbm, vmem, hbm, vmem, hbm, hbm, vmem, hbm, hbm],
        out_specs=(vmem, vmem),
        scratch_shapes=[
            pltpu.VMEM((TILES, F), BF16),
            pltpu.VMEM((F, D), BF16),
            pltpu.VMEM((D, 3 * D), BF16),
            pltpu.VMEM((D, D), BF16),
            pltpu.VMEM((D, FF), BF16),
            pltpu.VMEM((FF, D), BF16),
            pltpu.VMEM((3 * D, D), BF16),
            pltpu.VMEM((TILES, D), BF16),
            pltpu.VMEM((TILES, D), BF16),
            pltpu.VMEM((TILES, 128), F32),
            pltpu.VMEM((DEVICES, 16, 384), BF16),
            pltpu.VMEM((DEVICES, 16, 384), BF16),
            pltpu.VMEM((ROWS, RATE, D), BF16),
            pltpu.VMEM((ROWS, RATE, 128), BF16),
            pltpu.VMEM((HEADS, 128, SLOTS), BF16),
            pltpu.VMEM((HEADS // 2, SLOTS, 128), BF16),
            pltpu.VMEM((HEADS, 64, SLOTS), BF16),
            pltpu.VMEM((2, SLOTS, QUERIES), F32),
            pltpu.VMEM((HEADS, 64, SLOTS), F32),
            pltpu.VMEM((HEADS, 8, SLOTS), F32),
            pltpu.VMEM((D, SLOTS), BF16),
            pltpu.VMEM((HEADS, 32, 128), BF16),
            pltpu.VMEM((N_SEQ, 32, 128), BF16),
            pltpu.VMEM((N_SEQ, ROWS, 128), F32),
            pltpu.VMEM((HEADS, ROWS, 128), F32),
            pltpu.VMEM((128, SLOTS), F32),
            pltpu.VMEM((3, DEVICES, 16, 128), BF16),
            pltpu.VMEM((3, DEVICES, 16, 128), BF16),
            pltpu.VMEM((TILES, D), F32),
            pltpu.VMEM((TILES, D), F32),
            dma((6,)),
            dma,
            dma((DEVICES,)),
            dma,
            dma((N_SEQ,)),
            dma,
            dma((HEADS,)),
            dma((3,)),
            dma((3, DEVICES)),
        ],
        compiler_params=pltpu.CompilerParams(collective_id=0, has_side_effects=True, vmem_limit_bytes=62 << 20),
    )(
        tile_feats, tile_dest, embed_weight, norm1_gain.reshape(1, D), qkv_weight, out_weight,
        norm2_gain.reshape(1, D), up_weight, down_weight,
    )
    return tile_out, far_heads[None]


def solution(mesh):
    return jax.shard_map(
        on_device,
        mesh=mesh,
        in_specs=(P(("dp", "seq"), None), P(("dp", "seq"), None), P(), P(), P(), P(), P(), P(), P()),
        out_specs=(P(("dp", "seq"), None), P("dp", None, "seq", None)),
        check_vma=False,
    )
```

```python
import functools
import math

import jax
import jax.numpy as jnp
from jax import lax
from jax.experimental import pallas as pl
from jax.experimental.pallas import tpu as pltpu
from jax.sharding import PartitionSpec as P

F32 = jnp.float32
BF16 = jnp.bfloat16
MESH = pl.DeviceIdType.MESH
HEADS = 16
HEAD = 48
D = 768
F = 1536
FF = 3072
TILES = 512
SLOTS = 1024
CAP = 8
N_DP = 4
N_SEQ = 32
DEVICES = 128
RATE = 64
ROWS = SLOTS // RATE
QUERIES = 512
FF_BLOCK = 512
EPSILON = 1e-5
MASKED = -1e30
EMPTY = 1e30
SCALE = HEAD ** -0.5 * math.log2(math.e)
NT = (((1,), (1,)), ((), ()))
TN = (((0,), (0,)), ((), ()))


def dot(a, b):
    return jnp.dot(a, b, preferred_element_type=F32)


def iota(shape, axis):
    return lax.broadcasted_iota(jnp.int32, shape, axis)


def layer_norm(x, gain):
    centred = x - jnp.mean(x, axis=1, keepdims=True)
    spread = jnp.mean(centred * centred, axis=1, keepdims=True)
    return (centred * lax.rsqrt(spread + EPSILON) * gain).astype(BF16)


def to_message(rows):
    n, w = rows.shape
    left = rows[:, : w // 2].reshape(n // CAP, CAP, w // 2)
    right = rows[:, w // 2 :].reshape(n // CAP, CAP, w // 2)
    return jnp.concatenate([left, right], axis=1).astype(BF16)


def from_message(message):
    n, _, w = message.shape
    wide = message.astype(F32)
    left = wide[:, :CAP].reshape(n * CAP, w)
    right = wide[:, CAP:].reshape(n * CAP, w)
    return jnp.concatenate([left, right], axis=1)


def kernel(
    feats_hbm, dest_ref, embed_hbm, gain1_ref, qkv_hbm, out_hbm, gain2_ref, up_hbm, down_hbm,
    tile_ref, far_ref,
    feats, embed_w, qkv_w, out_w, up_w, down_w, qkv_t,
    embedded, normed, slot_col, send1, recv1, x_ref, bias_ref,
    q_t, k_ref, v_t, scores, near, peak, mixed,
    far_send, far_recv, res_send, res_recv, far_t,
    send2, recv2, hidden, total,
    load_sem, send1_sem, recv1_sem, fsend_sem, frecv_sem, rsend_sem, rrecv_sem, send2_sem, recv2_sem, keep_sem,
):
    dp, sq = lax.axis_index("dp"), lax.axis_index("seq")
    me = dp * N_SEQ + sq

    x0, z0, y0, c0 = dp, sq // 8, lax.rem(sq // 2, 4), lax.rem(sq, 2)
    x_up = [lax.rem(x0 + i, 4) for i in range(4)]
    x_down = [lax.rem(x0 + 4 - i, 4) for i in range(4)]
    z_up = [lax.rem(z0 + i, 4) for i in range(4)]
    place = lax.rem(sq, 8)
    places = [lax.rem(y0 + i // 2, 4) * 2 + lax.rem(c0 + i, 2) for i in range(8)]

    def each_partner(t, forward, act, skip_self):
        for i in range(4):
            turn = lax.rem(i + t + 1, 4)
            x = x_up[i] if forward else x_down[i]
            z = lax.rem(z0 + turn, 4) if forward else lax.rem(z0 + 4 - turn, 4)
            for j in range(8):
                if not (skip_self and i == 0 and j == 0):
                    act(4 * t + i, x, z * 8 + places[j], places[j])

    def all_partners(forward, act):
        def some(t, carry):
            each_partner(t, forward, act, False)
            return carry

        lax.fori_loop(0, 3, some, 0)
        each_partner(3, forward, act, True)

    def unit_of(j):
        i = (x0 + 4 - (j >> 2)) & 3
        return (((z0 - (j & 3) + 8 - i - 1) & 3) << 2) + i

    loads = [
        pltpu.make_async_copy(src, dst, load_sem.at[i])
        for i, (src, dst) in enumerate(
            [(feats_hbm, feats), (embed_hbm, embed_w), (qkv_hbm, qkv_w), (out_hbm, out_w), (up_hbm, up_w), (down_hbm, down_w)]
        )
    ]
    for load in loads:
        load.start()

    barrier = pltpu.get_barrier_semaphore()

    def greet(unit, x, s, p):
        pl.semaphore_signal(barrier, inc=1, device_id=(x, s), device_id_type=MESH)

    all_partners(True, greet)

    dest = dest_ref[...]
    onehot = (dest == iota((DEVICES, TILES), 0)).astype(F32)
    before = (iota((TILES, TILES), 0) < iota((TILES, TILES), 1)).astype(BF16)
    rank = jnp.sum(dot(onehot.astype(BF16), before) * onehot, axis=0, keepdims=True)
    slots = dest.astype(F32) * CAP + rank
    slot_col[...] = jnp.transpose(jnp.broadcast_to(slots, (128, TILES)))
    slot_row = slots.astype(jnp.int32)

    loads[0].wait()
    loads[1].wait()
    for i in range(4):
        rows = pl.ds(i * 128, 128)
        tile_rows = dot(feats[rows, :], embed_w[...]).astype(BF16)
        embedded[rows, :] = tile_rows
        normed[rows, :] = layer_norm(tile_rows.astype(F32), gain1_ref[...].reshape(1, D))

    def pack(i, carry):
        chosen = (iota((256, TILES), 0) + i * 256 == slot_row).astype(F32)
        rows = dot(chosen.astype(BF16), normed[...])
        used = jnp.sum(chosen, axis=1, keepdims=True)
        first = jnp.where((iota((256, 128), 1) == 0) & (used < 0.5), EMPTY, rows[:, :128])
        send1[pl.ds(i * 32, 32)] = to_message(jnp.concatenate([first, rows[:, 128:]], axis=1))
        return carry

    lax.fori_loop(0, 4, pack, 0)
    pl.semaphore_wait(barrier, DEVICES - 1)

    def send_rows(unit, x, s, p):
        pltpu.make_async_remote_copy(
            src_ref=send1.at[x * N_SEQ + s], dst_ref=recv1.at[unit * 8 + place], send_sem=send1_sem,
            recv_sem=recv1_sem.at[unit // 4], device_id=(x, s), device_id_type=MESH,
        ).start()

    all_partners(True, send_rows)
    pltpu.make_async_copy(send1.at[me], recv1.at[12 * 8 + place], recv1_sem.at[3]).start()

    loads[2].wait()

    def turn(i, carry):
        columns = pl.ds(pl.multiple_of(i * 128, 128), 128)
        qkv_t[columns, :] = jnp.transpose(qkv_w[:, columns].astype(F32)).astype(BF16)
        return carry

    lax.fori_loop(0, 3 * D // 128, turn, 0)
    one_row = (iota((16, SLOTS), 0) == 0).astype(BF16)
    for h in range(HEADS):
        base = 64 * (h % 2)
        q_t[h, pl.ds(64 - base, 64), :] = jnp.zeros((64, SLOTS), BF16)
        q_t[h, pl.ds(base + HEAD, 16), :] = one_row
        v_t[h, pl.ds(HEAD, 16), :] = jnp.ones((16, SLOTS), BF16)

    def project(g, carry):
        group = recv1.at[pl.ds(g * 32, 32)]
        pltpu.make_async_copy(group, group, recv1_sem.at[g]).wait()
        rows = from_message(recv1[pl.ds(g * 32, 32)])
        empty = rows[:, 0:1] > 0.1 * EMPTY
        rows = jnp.where(empty, 0.0, rows).astype(BF16)
        bias = jnp.broadcast_to(jnp.where(empty, MASKED, 0.0), (256, 128))
        x_ref[pl.ds(g * 4, 4)] = rows.reshape(4, RATE, D)
        bias_ref[pl.ds(g * 4, 4)] = bias.astype(BF16).reshape(4, RATE, 128)
        lanes = pl.ds(pl.multiple_of(g * 256, 256), 256)
        query = (lax.dot_general(qkv_t[0:D, :], rows, NT, preferred_element_type=F32) * SCALE).astype(BF16)
        for h in range(HEADS):
            q_t[h, pl.ds(64 * (h % 2), HEAD), lanes] = query[h * HEAD : (h + 1) * HEAD]
        key = lax.dot_general(qkv_t[D : 2 * D, :], rows, NT, preferred_element_type=F32)
        masks = jnp.where(iota((16, 256), 0) == 0, jnp.transpose(bias)[0:16, :], 0.0)
        for p in range(HEADS // 2):
            pair = jnp.concatenate(
                [key[96 * p : 96 * p + 48], masks, key[96 * p + 48 : 96 * p + 96], masks], axis=0
            )
            k_ref[p, pl.ds(pl.multiple_of(g * 256, 256), 256), :] = jnp.transpose(pair).astype(BF16)
        value = lax.dot_general(qkv_t[2 * D :, :], rows, NT, preferred_element_type=F32).astype(BF16)
        for h in range(HEADS):
            v_t[h, pl.ds(0, HEAD), lanes] = value[h * HEAD : (h + 1) * HEAD]
        return carry

    lax.fori_loop(0, 4, project, 0)

    rows = x_ref[:, pl.ds(0, 16), :].reshape(256, D)
    row = iota((256, 256), 0)
    swap = (iota((256, 256), 1) == unit_of(row & 15) * 16 + (row >> 4)).astype(BF16)
    rows = dot(swap, rows).astype(BF16)
    bias = dot(swap, bias_ref[:, pl.ds(0, 16), :].reshape(256, 128))
    low = HEAD * (iota((256, D), 0) >> 4)
    column = iota((256, D), 1)
    own = (column >= low) & (column < low + HEAD)
    turns = (iota((D, 128), 0) - iota((D, 128), 1)).astype(F32) * (1.0 / HEAD)
    whole = jnp.abs(turns - jnp.round(turns)) < 0.01
    lane = iota((D, 128), 1)
    to_front = (whole & (lane < HEAD)).astype(BF16)
    turns = turns + (64.0 / HEAD)
    whole = jnp.abs(turns - jnp.round(turns)) < 0.01
    to_back = (whole & (lane >= 64) & (lane < 64 + HEAD)).astype(BF16)

    def own_head(part, scale):
        product = dot(rows, qkv_w[:, part * D : (part + 1) * D]) * scale
        return jnp.where(own, product, 0.0).astype(BF16)

    lane = iota((256, 128), 1)
    far_q = jnp.where(lane == HEAD, 1.0, dot(own_head(0, SCALE), to_front))
    far_kv = dot(own_head(1, 1.0), to_front) + dot(own_head(2, 1.0), to_back)
    far_kv = jnp.where(lane == HEAD, bias, jnp.where(lane == 64 + HEAD, 1.0, far_kv))
    far_send[...] = jnp.concatenate(
        [far_q.reshape(HEADS, ROWS, 128), far_kv.reshape(HEADS, ROWS, 128)], axis=1
    ).astype(BF16)

    mine = sq // 2
    for i in range(1, HEADS):
        h = lax.rem(mine + i, HEADS)
        pltpu.make_async_remote_copy(
            src_ref=far_send.at[h], dst_ref=far_recv.at[sq], send_sem=fsend_sem, recv_sem=frecv_sem.at[sq],
            device_id=(dp, 2 * h), device_id_type=MESH,
        ).start()

    @pl.when(c0 == 1)
    def _():
        pltpu.make_async_remote_copy(
            src_ref=far_send.at[mine], dst_ref=far_recv.at[sq], send_sem=fsend_sem, recv_sem=frecv_sem.at[sq],
            device_id=(dp, 2 * mine), device_id_type=MESH,
        ).start()

    @pl.when(c0 == 0)
    def _():
        pltpu.make_async_copy(far_send.at[mine], far_recv.at[sq], frecv_sem.at[sq]).start()

    parts = SLOTS // QUERIES

    def score(h, i):
        return lax.dot_general(
            k_ref[h // 2], q_t[h, :, i * QUERIES : (i + 1) * QUERIES], (((1,), (0,)), ((), ())), preferred_element_type=F32
        )

    def attend_head(h, act=None):
        for i in range(parts):
            if i + 1 < parts:
                later = score(h, i + 1)
            else:
                later = score(jnp.minimum(h + 1, HEADS - 1), 0)
            if act is not None and i == 0:
                act()
            block = scores[i % 2]
            top = jnp.max(block, axis=0, keepdims=True)
            weights = jnp.exp2(block - top).astype(BF16)
            near[h, :, i * QUERIES : (i + 1) * QUERIES] = dot(v_t[h], weights)
            peak[h, :, i * QUERIES : (i + 1) * QUERIES] = jnp.broadcast_to(top, (8, QUERIES))
            scores[(i + 1) % 2] = later

    def attend(first, last):
        def one_head(h, carry):
            attend_head(h)
            return carry

        lax.fori_loop(first, last, one_head, 0)

    def attend_and_send(first, c):
        def one_head(t, carry):
            attend_head(first + t, lambda: each_partner(t, False, send_back(c), False))
            return carry

        lax.fori_loop(0, 3, one_head, 0)
        attend_head(first + 3, lambda: each_partner(3, False, send_back(c), True))
        attend_head(first + 4)

    def far_branch():
        def arrived(s, carry):
            pltpu.make_async_copy(far_recv.at[s], far_recv.at[s], frecv_sem.at[s]).wait()
            return carry

        lax.fori_loop(0, N_SEQ, arrived, 0)
        queries = far_recv[:, pl.ds(0, 16), :].reshape(N_SEQ * ROWS, 128)
        pairs = far_recv[:, pl.ds(16, 16), :].reshape(N_SEQ * ROWS, 128)
        block = lax.dot_general(queries, pairs, NT, preferred_element_type=F32)
        top = jnp.max(block, axis=1, keepdims=True)
        result = dot(jnp.exp2(block - top).astype(BF16), pairs)
        summed = result[:, 64 + HEAD : 65 + HEAD]
        result = jnp.where(iota(result.shape, 1) < 64, top + jnp.log2(summed), result / summed)
        res_send[...] = result.reshape(N_SEQ, ROWS, 128)

        for i in range(1, N_SEQ):
            s = lax.rem(sq + i, N_SEQ)
            pltpu.make_async_remote_copy(
                src_ref=res_send.at[s], dst_ref=res_recv.at[mine], send_sem=rsend_sem, recv_sem=rrecv_sem.at[mine],
                device_id=(dp, s), device_id_type=MESH,
            ).start()
        pltpu.make_async_copy(res_send.at[sq], res_recv.at[mine], rrecv_sem.at[mine]).start()
        pltpu.make_async_copy(
            res_send.at[pl.ds(0, N_SEQ - 1)], res_send.at[pl.ds(0, N_SEQ - 1)], rsend_sem
        ).wait()

    def far_arrived():
        def arrived(h, carry):
            pltpu.make_async_copy(res_recv.at[h], res_recv.at[h], rrecv_sem.at[h]).wait()
            return carry

        lax.fori_loop(0, HEADS, arrived, 0)
        results = res_recv[...].reshape(HEADS * ROWS, 128)
        far_ref[...] = res_recv[:, :, 64 : 64 + HEAD]
        lane = iota((HEADS * ROWS, 128), 1)
        high = results.astype(BF16).astype(F32)
        middle = (results - high).astype(BF16).astype(F32)
        lowest = results - high - middle
        split = jnp.where(lane >= 64, results, jnp.where(lane == 0, high, jnp.where(lane == 1, middle, lowest)))
        row = iota((HEADS * ROWS, SLOTS), 0)
        spread = (iota((HEADS * ROWS, SLOTS), 1) == unit_of(row & 15) * RATE + (row >> 4)).astype(BF16)
        far_t[...] = lax.dot_general(split.astype(BF16), spread, TN, preferred_element_type=F32)

    def blend(first, last):
        def one_head(h, carry):
            summed = near[h, HEAD : HEAD + 1, :]
            near_lse = peak[h, 0:1, :] + jnp.log2(summed)
            far_lse = far_t[0:1, :] + far_t[1:2, :] + far_t[2:3, :]
            far_lse = jnp.where((iota((1, SLOTS), 1) & (RATE - 1)) == h, far_lse, MASKED)
            larger = jnp.maximum(near_lse, far_lse)
            near_weight = jnp.exp2(near_lse - larger)
            far_weight = jnp.exp2(far_lse - larger)
            both = near_weight + far_weight
            joined = near[h, 0:HEAD, :] * (near_weight / (both * summed)) + far_t[64 : 64 + HEAD, :] * (far_weight / both)
            mixed[pl.ds(pl.multiple_of(h * HEAD, 16), HEAD), :] = joined.astype(BF16)
            return carry

        lax.fori_loop(first, last, one_head, 0)

    def pack_back(c):
        def some(g, carry):
            lanes = pl.ds(pl.multiple_of(g * 256, 256), 256)
            rows = jnp.transpose(mixed[256 * c : 256 * (c + 1), lanes].astype(F32))
            send2[c, pl.ds(g * 32, 32)] = to_message(rows)
            return carry

        lax.fori_loop(0, 4, some, 0)
        pltpu.make_async_copy(send2.at[c, 12 * 8 + place], recv2.at[c, me], keep_sem.at[c]).start()

    def send_back(c):
        def act(unit, x, s, p):
            pltpu.make_async_remote_copy(
                src_ref=send2.at[c, unit * 8 + p], dst_ref=recv2.at[c, me], send_sem=send2_sem.at[c],
                recv_sem=recv2_sem.at[c], device_id=(x, s), device_id_type=MESH,
            ).start()

        return act

    scores[0] = score(0, 0)
    attend(0, 3)

    @pl.when(c0 == 0)
    def _():
        far_branch()

    attend(3, 6)
    far_arrived()
    blend(0, 6)
    pack_back(0)
    attend_and_send(6, 0)
    blend(6, 11)
    pack_back(1)
    attend_and_send(11, 1)
    blend(11, 16)
    pack_back(2)
    all_partners(False, send_back(2))

    loads[3].wait()
    hidden[...] = embedded[...].astype(F32)
    for c in range(3):
        pltpu.make_async_copy(send2.at[c, 12 * 8 + place], recv2.at[c, me], keep_sem.at[c]).wait()
        most = recv2.at[c, pl.ds(0, DEVICES - 1)]
        pltpu.make_async_copy(most, most, recv2_sem.at[c]).wait()
        taken = jnp.zeros((TILES, 256), F32)
        for g in range(4):
            chosen = (iota((TILES, 256), 1) + g * 256 == slot_col[:, 0:1].astype(jnp.int32)).astype(BF16)
            taken = taken + dot(chosen, from_message(recv2[c, pl.ds(g * 32, 32)]).astype(BF16))
        hidden[...] += dot(taken.astype(BF16), out_w[256 * c : 256 * (c + 1), :])
    loads[4].wait()
    loads[5].wait()
    state = hidden[...].astype(BF16).astype(F32)
    normed[...] = layer_norm(state, gain2_ref[...].reshape(1, D))
    total[...] = state

    def feed(i, carry):
        columns = pl.ds(pl.multiple_of(i * FF_BLOCK, FF_BLOCK), FF_BLOCK)
        inner = dot(normed[...], up_w[:, columns])
        inner = jax.nn.gelu(inner, approximate=True).astype(BF16)
        total[...] += dot(inner, down_w[columns, :])
        return carry

    lax.fori_loop(0, FF // FF_BLOCK, feed, 0)
    tile_ref[...] = total[...].astype(BF16)

    most = pl.ds(0, DEVICES - 1)
    pltpu.make_async_copy(send1.at[most], send1.at[most], send1_sem).wait()
    for c in range(3):
        pltpu.make_async_copy(send2.at[c, most], send2.at[c, most], send2_sem.at[c]).wait()

    @pl.when(c0 == 0)
    def _():
        pltpu.make_async_copy(far_send.at[pl.ds(0, 15)], far_send.at[pl.ds(0, 15)], fsend_sem).wait()

    @pl.when(c0 == 1)
    def _():
        pltpu.make_async_copy(far_send, far_send, fsend_sem).wait()


def on_device(tile_feats, tile_dest, embed_weight, norm1_gain, qkv_weight, out_weight, norm2_gain, up_weight, down_weight):
    hbm = pl.BlockSpec(memory_space=pl.ANY)
    vmem = pl.BlockSpec(memory_space=pltpu.VMEM)
    dma = pltpu.SemaphoreType.DMA
    tile_out, far_heads = pl.pallas_call(
        kernel,
        out_shape=(
            jax.ShapeDtypeStruct((TILES, D), BF16),
            jax.ShapeDtypeStruct((HEADS, ROWS, HEAD), F32),
        ),
        in_specs=[hbm, vmem, hbm, vmem, hbm, hbm, vmem, hbm, hbm],
        out_specs=(vmem, vmem),
        scratch_shapes=[
            pltpu.VMEM((TILES, F), BF16),
            pltpu.VMEM((F, D), BF16),
            pltpu.VMEM((D, 3 * D), BF16),
            pltpu.VMEM((D, D), BF16),
            pltpu.VMEM((D, FF), BF16),
            pltpu.VMEM((FF, D), BF16),
            pltpu.VMEM((3 * D, D), BF16),
            pltpu.VMEM((TILES, D), BF16),
            pltpu.VMEM((TILES, D), BF16),
            pltpu.VMEM((TILES, 128), F32),
            pltpu.VMEM((DEVICES, 16, 384), BF16),
            pltpu.VMEM((DEVICES, 16, 384), BF16),
            pltpu.VMEM((ROWS, RATE, D), BF16),
            pltpu.VMEM((ROWS, RATE, 128), BF16),
            pltpu.VMEM((HEADS, 128, SLOTS), BF16),
            pltpu.VMEM((HEADS // 2, SLOTS, 128), BF16),
            pltpu.VMEM((HEADS, 64, SLOTS), BF16),
            pltpu.VMEM((2, SLOTS, QUERIES), F32),
            pltpu.VMEM((HEADS, 64, SLOTS), F32),
            pltpu.VMEM((HEADS, 8, SLOTS), F32),
            pltpu.VMEM((D, SLOTS), BF16),
            pltpu.VMEM((HEADS, 32, 128), BF16),
            pltpu.VMEM((N_SEQ, 32, 128), BF16),
            pltpu.VMEM((N_SEQ, ROWS, 128), F32),
            pltpu.VMEM((HEADS, ROWS, 128), F32),
            pltpu.VMEM((128, SLOTS), F32),
            pltpu.VMEM((3, DEVICES, 16, 128), BF16),
            pltpu.VMEM((3, DEVICES, 16, 128), BF16),
            pltpu.VMEM((TILES, D), F32),
            pltpu.VMEM((TILES, D), F32),
            dma((6,)),
            dma,
            dma((4,)),
            dma,
            dma((N_SEQ,)),
            dma,
            dma((HEADS,)),
            dma((3,)),
            dma((3,)),
            dma((3,)),
        ],
        compiler_params=pltpu.CompilerParams(collective_id=0, has_side_effects=True, vmem_limit_bytes=62 << 20),
    )(
        tile_feats, tile_dest.reshape(1, TILES), embed_weight, norm1_gain, qkv_weight, out_weight,
        norm2_gain, up_weight, down_weight,
    )
    return tile_out, far_heads[None]


def solution(mesh):
    return jax.shard_map(
        on_device,
        mesh=mesh,
        in_specs=(P(("dp", "seq"), None), P(("dp", "seq"), None), P(), P(), P(), P(), P(), P(), P()),
        out_specs=(P(("dp", "seq"), None), P("dp", None, "seq", None)),
        check_vma=False,
    )
```

```python
import functools
import math

import jax
import jax.numpy as jnp
from jax import lax
from jax.experimental import pallas as pl
from jax.experimental.pallas import tpu as pltpu
from jax.sharding import PartitionSpec as P

F32 = jnp.float32
BF16 = jnp.bfloat16
MESH = pl.DeviceIdType.MESH
HEADS = 16
HEAD = 48
D = 768
F = 1536
FF = 3072
TILES = 512
SLOTS = 1024
CAP = 8
N_DP = 4
N_SEQ = 32
DEVICES = 128
RATE = 64
ROWS = SLOTS // RATE
QUERIES = 512
FF_BLOCK = 512
EPSILON = 1e-5
MASKED = -1e30
EMPTY = 1e30
SCALE = HEAD ** -0.5 * math.log2(math.e)
NT = (((1,), (1,)), ((), ()))
TN = (((0,), (0,)), ((), ()))


def dot(a, b):
    return jnp.dot(a, b, preferred_element_type=F32)


def iota(shape, axis):
    return lax.broadcasted_iota(jnp.int32, shape, axis)


def layer_norm(x, gain):
    centred = x - jnp.mean(x, axis=1, keepdims=True)
    spread = jnp.mean(centred * centred, axis=1, keepdims=True)
    return (centred * lax.rsqrt(spread + EPSILON) * gain).astype(BF16)


def to_message(rows):
    n, w = rows.shape
    left = rows[:, : w // 2].reshape(n // CAP, CAP, w // 2)
    right = rows[:, w // 2 :].reshape(n // CAP, CAP, w // 2)
    return jnp.concatenate([left, right], axis=1).astype(BF16)


def from_message(message):
    n, _, w = message.shape
    wide = message.astype(F32)
    left = wide[:, :CAP].reshape(n * CAP, w)
    right = wide[:, CAP:].reshape(n * CAP, w)
    return jnp.concatenate([left, right], axis=1)


def kernel(
    feats_hbm, dest_ref, embed_hbm, gain1_ref, qkv_hbm, out_hbm, gain2_ref, up_hbm, down_hbm,
    tile_ref, far_ref,
    feats, embed_w, qkv_w, out_w, up_w, down_w, qkv_t,
    embedded, normed, slot_col, send1, recv1,
    q_t, k_ref, v_t, scores, near, peak, mixed,
    far_cols, far_send, far_recv, res_send, res_recv, far_t,
    send2, recv2, hidden, total,
    load_sem, send1_sem, recv1_sem, fsend_sem, frecv_sem, rsend_sem, rrecv_sem, send2_sem, recv2_sem, keep_sem,
):
    dp, sq = lax.axis_index("dp"), lax.axis_index("seq")
    me = dp * N_SEQ + sq

    x0, z0, y0, c0 = dp, sq // 8, lax.rem(sq // 2, 4), lax.rem(sq, 2)
    x_up = [lax.rem(x0 + i, 4) for i in range(4)]
    x_down = [lax.rem(x0 + 4 - i, 4) for i in range(4)]
    z_up = [lax.rem(z0 + i, 4) for i in range(4)]
    place = lax.rem(sq, 8)
    places = [lax.rem(y0 + i // 2, 4) * 2 + lax.rem(c0 + i, 2) for i in range(8)]

    def each_partner(t, forward, act, skip_self):
        for i in range(4):
            turn = lax.rem(i + t + 1, 4)
            x = x_up[i] if forward else x_down[i]
            z = lax.rem(z0 + turn, 4) if forward else lax.rem(z0 + 4 - turn, 4)
            for j in range(8):
                if not (skip_self and i == 0 and j == 0):
                    act(4 * t + i, x, z * 8 + places[j], places[j])

    def all_partners(forward, act):
        def some(t, carry):
            each_partner(t, forward, act, False)
            return carry

        lax.fori_loop(0, 3, some, 0)
        each_partner(3, forward, act, True)

    def unit_of(j):
        i = (x0 + 4 - (j >> 2)) & 3
        return (((z0 - (j & 3) + 8 - i - 1) & 3) << 2) + i

    loads = [
        pltpu.make_async_copy(src, dst, load_sem.at[i])
        for i, (src, dst) in enumerate(
            [(feats_hbm, feats), (embed_hbm, embed_w), (qkv_hbm, qkv_w), (out_hbm, out_w), (up_hbm, up_w), (down_hbm, down_w)]
        )
    ]
    for load in loads:
        load.start()

    barrier = pltpu.get_barrier_semaphore()

    def greet(unit, x, s, p):
        pl.semaphore_signal(barrier, inc=1, device_id=(x, s), device_id_type=MESH)

    all_partners(True, greet)

    dest = dest_ref[...]
    onehot = (dest == iota((DEVICES, TILES), 0)).astype(F32)
    before = (iota((TILES, TILES), 0) < iota((TILES, TILES), 1)).astype(BF16)
    rank = jnp.sum(dot(onehot.astype(BF16), before) * onehot, axis=0, keepdims=True)
    slots = dest.astype(F32) * CAP + rank
    slot_col[...] = jnp.transpose(jnp.broadcast_to(slots, (128, TILES)))
    slot_row = slots.astype(jnp.int32)

    loads[0].wait()
    loads[1].wait()
    for i in range(4):
        rows = pl.ds(i * 128, 128)
        tile_rows = dot(feats[rows, :], embed_w[...]).astype(BF16)
        embedded[rows, :] = tile_rows
        normed[rows, :] = layer_norm(tile_rows.astype(F32), gain1_ref[...].reshape(1, D))

    def pack(i, carry):
        chosen = (iota((256, TILES), 0) + i * 256 == slot_row).astype(F32)
        rows = dot(chosen.astype(BF16), normed[...])
        used = jnp.sum(chosen, axis=1, keepdims=True)
        first = jnp.where((iota((256, 128), 1) == 0) & (used < 0.5), EMPTY, rows[:, :128])
        send1[pl.ds(i * 32, 32)] = to_message(jnp.concatenate([first, rows[:, 128:]], axis=1))
        return carry

    lax.fori_loop(0, 4, pack, 0)
    pl.semaphore_wait(barrier, DEVICES - 1)

    def send_rows(unit, x, s, p):
        pltpu.make_async_remote_copy(
            src_ref=send1.at[x * N_SEQ + s], dst_ref=recv1.at[unit * 8 + place], send_sem=send1_sem,
            recv_sem=recv1_sem.at[unit // 4], device_id=(x, s), device_id_type=MESH,
        ).start()

    all_partners(True, send_rows)
    pltpu.make_async_copy(send1.at[me], recv1.at[12 * 8 + place], recv1_sem.at[3]).start()

    loads[2].wait()

    def turn(i, carry):
        columns = pl.ds(pl.multiple_of(i * 128, 128), 128)
        qkv_t[columns, :] = jnp.transpose(qkv_w[:, columns].astype(F32)).astype(BF16)
        return carry

    lax.fori_loop(0, 3 * D // 128, turn, 0)
    one_row = (iota((16, SLOTS), 0) == 0).astype(BF16)
    for h in range(HEADS):
        base = 64 * (h % 2)
        q_t[h, pl.ds(64 - base, 64), :] = jnp.zeros((64, SLOTS), BF16)
        q_t[h, pl.ds(base + HEAD, 16), :] = one_row
        v_t[h, pl.ds(HEAD, 16), :] = jnp.ones((16, SLOTS), BF16)

    def project(g, carry):
        group = recv1.at[pl.ds(g * 32, 32)]
        pltpu.make_async_copy(group, group, recv1_sem.at[g]).wait()
        rows = from_message(recv1[pl.ds(g * 32, 32)])
        empty = rows[:, 0:1] > 0.1 * EMPTY
        rows = jnp.where(empty, 0.0, rows).astype(BF16)
        bias = jnp.broadcast_to(jnp.where(empty, MASKED, 0.0), (256, 128))
        lanes = pl.ds(pl.multiple_of(g * 256, 256), 256)
        query = (lax.dot_general(qkv_t[0:D, :], rows, NT, preferred_element_type=F32) * SCALE).astype(BF16)
        for h in range(HEADS):
            q_t[h, pl.ds(64 * (h % 2), HEAD), lanes] = query[h * HEAD : (h + 1) * HEAD]
        key = lax.dot_general(qkv_t[D : 2 * D, :], rows, NT, preferred_element_type=F32)
        masks = jnp.where(iota((16, 256), 0) == 0, jnp.transpose(bias)[0:16, :], 0.0)
        for p in range(HEADS // 2):
            pair = jnp.concatenate(
                [key[96 * p : 96 * p + 48], masks, key[96 * p + 48 : 96 * p + 96], masks], axis=0
            )
            k_ref[p, pl.ds(pl.multiple_of(g * 256, 256), 256), :] = jnp.transpose(pair).astype(BF16)
        value = lax.dot_general(qkv_t[2 * D :, :], rows, NT, preferred_element_type=F32).astype(BF16)
        for h in range(HEADS):
            v_t[h, pl.ds(0, HEAD), lanes] = value[h * HEAD : (h + 1) * HEAD]
        lane, column = iota((256, 256), 0), iota((256, 256), 1)
        taken = ((lane & (RATE - 1)) == (column >> 4)) & (g * 4 + (lane >> 6) == unit_of(column & 15))
        taken = taken.astype(BF16)
        owner = iota((HEAD, 256), 1) >> 4
        for n, part in enumerate((query, key.astype(BF16), value)):
            wide = dot(part, taken)
            own = jnp.zeros((HEAD, 256), F32)
            for h in range(HEADS):
                own = own + jnp.where(owner == h, wide[h * HEAD : (h + 1) * HEAD], 0.0)
            far_cols[n * HEAD : (n + 1) * HEAD, :] += own
        far_cols[3 * HEAD :, :] += dot(masks.astype(BF16), taken)
        return carry

    far_cols[...] = jnp.zeros_like(far_cols)
    lax.fori_loop(0, 4, project, 0)

    one = jnp.where(iota((16, 256), 0) == 0, 1.0, 0.0)
    far_q = jnp.concatenate([far_cols[0:HEAD, :], one, jnp.zeros((64, 256), F32)], axis=0)
    far_kv = jnp.concatenate(
        [far_cols[HEAD : 2 * HEAD, :], far_cols[3 * HEAD :, :], far_cols[2 * HEAD : 3 * HEAD, :], one], axis=0
    )
    far_send[...] = jnp.concatenate(
        [jnp.transpose(far_q).reshape(HEADS, ROWS, 128), jnp.transpose(far_kv).reshape(HEADS, ROWS, 128)], axis=1
    ).astype(BF16)

    mine = sq // 2

    def send_far(h, s):
        pltpu.make_async_remote_copy(
            src_ref=far_send.at[h], dst_ref=far_recv.at[sq], send_sem=fsend_sem, recv_sem=frecv_sem,
            device_id=(dp, s), device_id_type=MESH,
        ).start()

    for i in range(1, HEADS):
        h = lax.rem(mine + i, HEADS)
        send_far(h, 2 * h)
        send_far(h, 2 * h + 1)
    send_far(mine, 2 * mine + 1 - c0)
    pltpu.make_async_copy(far_send.at[mine], far_recv.at[sq], frecv_sem).start()

    parts = SLOTS // QUERIES

    def score(h, i):
        return lax.dot_general(
            k_ref[h // 2], q_t[h, :, i * QUERIES : (i + 1) * QUERIES], (((1,), (0,)), ((), ())), preferred_element_type=F32
        )

    def attend_head(h, act=None):
        for i in range(parts):
            if i + 1 < parts:
                later = score(h, i + 1)
            else:
                later = score(jnp.minimum(h + 1, HEADS - 1) if not isinstance(h, int) else min(h + 1, HEADS - 1), 0)
            if act is not None and i == 0:
                act()
            block = scores[i % 2]
            top = jnp.max(block, axis=0, keepdims=True)
            weights = jnp.exp2(block - top).astype(BF16)
            near[h, :, i * QUERIES : (i + 1) * QUERIES] = dot(v_t[h], weights)
            peak[h, :, i * QUERIES : (i + 1) * QUERIES] = jnp.broadcast_to(top, (8, QUERIES))
            scores[(i + 1) % 2] = later

    def attend(first, last):
        for h in range(first, last):
            attend_head(h)

    def attend_and_send(first, c):
        def one_head(t, carry):
            attend_head(first + t, lambda: each_partner(t, False, send_back(c), False))
            return carry

        lax.fori_loop(0, 3, one_head, 0)
        attend_head(first + 3, lambda: each_partner(3, False, send_back(c), True))
        attend_head(first + 4)

    def far_branch():
        pltpu.make_async_copy(far_recv, far_recv, frecv_sem).wait()
        half = N_SEQ // 2
        queries = far_recv[pl.ds(half * c0, half), pl.ds(0, 16), :].reshape(half * ROWS, 128)
        pairs = far_recv[:, pl.ds(16, 16), :].reshape(N_SEQ * ROWS, 128)
        block = lax.dot_general(queries, pairs, NT, preferred_element_type=F32)
        top = jnp.max(block, axis=1, keepdims=True)
        result = dot(jnp.exp2(block - top).astype(BF16), pairs)
        summed = result[:, 64 + HEAD : 65 + HEAD]
        result = jnp.where(iota(result.shape, 1) < 64, top + jnp.log2(summed), result / summed)
        res_send[...] = result.reshape(half, ROWS, 128)

        def answer(i):
            to = lax.rem(sq + i, half)
            pltpu.make_async_remote_copy(
                src_ref=res_send.at[to], dst_ref=res_recv.at[mine], send_sem=rsend_sem, recv_sem=rrecv_sem,
                device_id=(dp, half * c0 + to), device_id_type=MESH,
            ).start()

        for i in range(1, half):
            answer(i)

        @pl.when(sq // half != c0)
        def _():
            answer(0)

        @pl.when(sq // half == c0)
        def _():
            pltpu.make_async_copy(res_send.at[lax.rem(sq, half)], res_recv.at[mine], rrecv_sem).start()

    def far_arrived():
        pltpu.make_async_copy(res_recv, res_recv, rrecv_sem).wait()
        results = res_recv[...].reshape(HEADS * ROWS, 128)
        far_ref[...] = res_recv[:, :, 64 : 64 + HEAD]
        lane = iota((HEADS * ROWS, 128), 1)
        high = results.astype(BF16).astype(F32)
        middle = (results - high).astype(BF16).astype(F32)
        lowest = results - high - middle
        split = jnp.where(lane >= 64, results, jnp.where(lane == 0, high, jnp.where(lane == 1, middle, lowest)))
        row = iota((HEADS * ROWS, SLOTS), 0)
        spread = (iota((HEADS * ROWS, SLOTS), 1) == unit_of(row & 15) * RATE + (row >> 4)).astype(BF16)
        far_t[...] = lax.dot_general(split.astype(BF16), spread, TN, preferred_element_type=F32)

    def blend(first, last):
        def one_head(h, carry):
            summed = near[h, HEAD : HEAD + 1, :]
            near_lse = peak[h, 0:1, :] + jnp.log2(summed)
            far_lse = far_t[0:1, :] + far_t[1:2, :] + far_t[2:3, :]
            far_lse = jnp.where((iota((1, SLOTS), 1) & (RATE - 1)) == h, far_lse, MASKED)
            larger = jnp.maximum(near_lse, far_lse)
            near_weight = jnp.exp2(near_lse - larger)
            far_weight = jnp.exp2(far_lse - larger)
            both = near_weight + far_weight
            joined = near[h, 0:HEAD, :] * (near_weight / (both * summed)) + far_t[64 : 64 + HEAD, :] * (far_weight / both)
            mixed[pl.ds(pl.multiple_of(h * HEAD, 16), HEAD), :] = joined.astype(BF16)
            return carry

        lax.fori_loop(first, last, one_head, 0)

    def pack_back(c):
        def some(g, carry):
            lanes = pl.ds(pl.multiple_of(g * 256, 256), 256)
            rows = jnp.transpose(mixed[256 * c : 256 * (c + 1), lanes].astype(F32))
            send2[c, pl.ds(g * 32, 32)] = to_message(rows)
            return carry

        lax.fori_loop(0, 4, some, 0)
        pltpu.make_async_copy(send2.at[c, 12 * 8 + place], recv2.at[c, me], keep_sem.at[c]).start()

    def send_back(c):
        def act(unit, x, s, p):
            pltpu.make_async_remote_copy(
                src_ref=send2.at[c, unit * 8 + p], dst_ref=recv2.at[c, me], send_sem=send2_sem.at[c],
                recv_sem=recv2_sem.at[c], device_id=(x, s), device_id_type=MESH,
            ).start()

        return act

    scores[0] = score(0, 0)
    attend(0, 3)
    far_branch()
    attend(3, 6)
    far_arrived()
    blend(0, 6)
    pack_back(0)
    attend_and_send(6, 0)
    blend(6, 11)
    pack_back(1)
    attend_and_send(11, 1)
    blend(11, 16)
    pack_back(2)
    all_partners(False, send_back(2))

    loads[3].wait()
    hidden[...] = embedded[...].astype(F32)
    for c in range(3):
        pltpu.make_async_copy(send2.at[c, 12 * 8 + place], recv2.at[c, me], keep_sem.at[c]).wait()
        most = recv2.at[c, pl.ds(0, DEVICES - 1)]
        pltpu.make_async_copy(most, most, recv2_sem.at[c]).wait()
        taken = jnp.zeros((TILES, 256), F32)
        for g in range(4):
            chosen = (iota((TILES, 256), 1) + g * 256 == slot_col[:, 0:1].astype(jnp.int32)).astype(BF16)
            taken = taken + dot(chosen, from_message(recv2[c, pl.ds(g * 32, 32)]).astype(BF16))
        hidden[...] += dot(taken.astype(BF16), out_w[256 * c : 256 * (c + 1), :])
    loads[4].wait()
    loads[5].wait()
    state = hidden[...].astype(BF16).astype(F32)
    normed[...] = layer_norm(state, gain2_ref[...].reshape(1, D))
    total[...] = state

    def columns(i):
        return pl.ds(i * FF_BLOCK if isinstance(i, int) else pl.multiple_of(i * FF_BLOCK, FF_BLOCK), FF_BLOCK)

    def feed(i, slot, last):
        if not last:
            later = dot(normed[...], up_w[:, columns(i + 1)])
        inner = jax.nn.gelu(scores[slot, 0:TILES, :], approximate=True).astype(BF16)
        total[...] += dot(inner, down_w[columns(i), :])
        if not last:
            scores[1 - slot, 0:TILES, :] = later

    def feed_two(k, carry):
        feed(2 * k, 0, False)
        feed(2 * k + 1, 1, False)
        return carry

    scores[0, 0:TILES, :] = dot(normed[...], up_w[:, columns(0)])
    lax.fori_loop(0, FF // FF_BLOCK // 2 - 1, feed_two, 0)
    feed(FF // FF_BLOCK - 2, 0, False)
    feed(FF // FF_BLOCK - 1, 1, True)
    tile_ref[...] = total[...].astype(BF16)

    most = pl.ds(0, DEVICES - 1)
    pltpu.make_async_copy(send1.at[most], send1.at[most], send1_sem).wait()
    for c in range(3):
        pltpu.make_async_copy(send2.at[c, most], send2.at[c, most], send2_sem.at[c]).wait()

    most = far_recv.at[pl.ds(0, N_SEQ - 1)]
    pltpu.make_async_copy(most, most, fsend_sem).wait()

    @pl.when(sq // 16 == c0)
    def _():
        most = res_send.at[pl.ds(0, 15)]
        pltpu.make_async_copy(most, most, rsend_sem).wait()

    @pl.when(sq // 16 != c0)
    def _():
        pltpu.make_async_copy(res_send, res_send, rsend_sem).wait()


def on_device(tile_feats, tile_dest, embed_weight, norm1_gain, qkv_weight, out_weight, norm2_gain, up_weight, down_weight):
    hbm = pl.BlockSpec(memory_space=pl.ANY)
    vmem = pl.BlockSpec(memory_space=pltpu.VMEM)
    dma = pltpu.SemaphoreType.DMA
    tile_out, far_heads = pl.pallas_call(
        kernel,
        out_shape=(
            jax.ShapeDtypeStruct((TILES, D), BF16),
            jax.ShapeDtypeStruct((HEADS, ROWS, HEAD), F32),
        ),
        in_specs=[hbm, vmem, hbm, vmem, hbm, hbm, vmem, hbm, hbm],
        out_specs=(vmem, vmem),
        scratch_shapes=[
            pltpu.VMEM((TILES, F), BF16),
            pltpu.VMEM((F, D), BF16),
            pltpu.VMEM((D, 3 * D), BF16),
            pltpu.VMEM((D, D), BF16),
            pltpu.VMEM((D, FF), BF16),
            pltpu.VMEM((FF, D), BF16),
            pltpu.VMEM((3 * D, D), BF16),
            pltpu.VMEM((TILES, D), BF16),
            pltpu.VMEM((TILES, D), BF16),
            pltpu.VMEM((TILES, 128), F32),
            pltpu.VMEM((DEVICES, 16, 384), BF16),
            pltpu.VMEM((DEVICES, 16, 384), BF16),
            pltpu.VMEM((HEADS, 128, SLOTS), BF16),
            pltpu.VMEM((HEADS // 2, SLOTS, 128), BF16),
            pltpu.VMEM((HEADS, 64, SLOTS), BF16),
            pltpu.VMEM((2, SLOTS, QUERIES), F32),
            pltpu.VMEM((HEADS, 64, SLOTS), F32),
            pltpu.VMEM((HEADS, 8, SLOTS), F32),
            pltpu.VMEM((D, SLOTS), BF16),
            pltpu.VMEM((3 * HEAD + 16, 256), F32),
            pltpu.VMEM((HEADS, 32, 128), BF16),
            pltpu.VMEM((N_SEQ, 32, 128), BF16),
            pltpu.VMEM((N_SEQ // 2, ROWS, 128), F32),
            pltpu.VMEM((HEADS, ROWS, 128), F32),
            pltpu.VMEM((128, SLOTS), F32),
            pltpu.VMEM((3, DEVICES, 16, 128), BF16),
            pltpu.VMEM((3, DEVICES, 16, 128), BF16),
            pltpu.VMEM((TILES, D), F32),
            pltpu.VMEM((TILES, D), F32),
            dma((6,)),
            dma,
            dma((4,)),
            dma,
            dma,
            dma,
            dma,
            dma((3,)),
            dma((3,)),
            dma((3,)),
        ],
        compiler_params=pltpu.CompilerParams(collective_id=0, has_side_effects=True, vmem_limit_bytes=62 << 20),
    )(
        tile_feats, tile_dest.reshape(1, TILES), embed_weight, norm1_gain, qkv_weight, out_weight,
        norm2_gain, up_weight, down_weight,
    )
    return tile_out, far_heads[None]


def solution(mesh):
    return jax.shard_map(
        on_device,
        mesh=mesh,
        in_specs=(P(("dp", "seq"), None), P(("dp", "seq"), None), P(), P(), P(), P(), P(), P(), P()),
        out_specs=(P(("dp", "seq"), None), P("dp", None, "seq", None)),
        check_vma=False,
    )
```

```python
import functools
import math

import jax
import jax.numpy as jnp
from jax import lax
from jax.experimental import pallas as pl
from jax.experimental.pallas import tpu as pltpu
from jax.sharding import PartitionSpec as P

F32 = jnp.float32
BF16 = jnp.bfloat16
MESH = pl.DeviceIdType.MESH
HEADS = 16
HEAD = 48
D = 768
F = 1536
FF = 3072
TILES = 512
SLOTS = 1024
CAP = 8
N_DP = 4
N_SEQ = 32
DEVICES = 128
RATE = 64
ROWS = SLOTS // RATE
QUERIES = 512
FF_BLOCK = 512
EPSILON = 1e-5
MASKED = -1e30
EMPTY = 1e30
SCALE = HEAD ** -0.5 * math.log2(math.e)
NT = (((1,), (1,)), ((), ()))
TN = (((0,), (0,)), ((), ()))


def dot(a, b):
    return jnp.dot(a, b, preferred_element_type=F32)


def iota(shape, axis):
    return lax.broadcasted_iota(jnp.int32, shape, axis)


def layer_norm(x, gain):
    centred = x - jnp.mean(x, axis=1, keepdims=True)
    spread = jnp.mean(centred * centred, axis=1, keepdims=True)
    return (centred * lax.rsqrt(spread + EPSILON) * gain).astype(BF16)


def to_message(rows):
    n, w = rows.shape
    left = rows[:, : w // 2].reshape(n // CAP, CAP, w // 2)
    right = rows[:, w // 2 :].reshape(n // CAP, CAP, w // 2)
    return jnp.concatenate([left, right], axis=1).astype(BF16)


def from_message(message):
    n, _, w = message.shape
    wide = message.astype(F32)
    left = wide[:, :CAP].reshape(n * CAP, w)
    right = wide[:, CAP:].reshape(n * CAP, w)
    return jnp.concatenate([left, right], axis=1)


def kernel(
    feats_hbm, dest_ref, embed_hbm, gain1_ref, qkv_hbm, out_hbm,
    state_ref, results_ref,
    feats, embed_w, qkv_w, out_w, qkv_t,
    embedded, normed, slot_col, send1, recv1,
    q_t, k_ref, v_t, scores, near, peak, mixed,
    far_cols, far_send, far_recv, res_send, res_recv, far_t,
    send2, recv2, hidden,
    load_sem, send1_sem, recv1_sem, fsend_sem, frecv_sem, rsend_sem, rrecv_sem, send2_sem, recv2_sem, keep_sem,
):
    dp, sq = lax.axis_index("dp"), lax.axis_index("seq")
    me = dp * N_SEQ + sq

    x0, z0, y0, c0 = dp, sq // 8, lax.rem(sq // 2, 4), lax.rem(sq, 2)
    x_up = [lax.rem(x0 + i, 4) for i in range(4)]
    x_down = [lax.rem(x0 + 4 - i, 4) for i in range(4)]
    z_up = [lax.rem(z0 + i, 4) for i in range(4)]
    place = lax.rem(sq, 8)
    places = [lax.rem(y0 + i // 2, 4) * 2 + lax.rem(c0 + i, 2) for i in range(8)]

    def each_partner(t, forward, act, skip_self):
        for i in range(4):
            turn = lax.rem(i + t + 1, 4)
            x = x_up[i] if forward else x_down[i]
            z = lax.rem(z0 + turn, 4) if forward else lax.rem(z0 + 4 - turn, 4)
            for j in range(8):
                if not (skip_self and i == 0 and j == 0):
                    act(4 * t + i, x, z * 8 + places[j], places[j])

    def all_partners(forward, act):
        def some(t, carry):
            each_partner(t, forward, act, False)
            return carry

        lax.fori_loop(0, 3, some, 0)
        each_partner(3, forward, act, True)

    def unit_of(j):
        i = (x0 + 4 - (j >> 2)) & 3
        return (((z0 - (j & 3) + 8 - i - 1) & 3) << 2) + i

    loads = [
        pltpu.make_async_copy(src, dst, load_sem.at[i])
        for i, (src, dst) in enumerate(
            [(feats_hbm, feats), (embed_hbm, embed_w), (qkv_hbm, qkv_w), (out_hbm, out_w)]
        )
    ]
    for load in loads:
        load.start()

    barrier = pltpu.get_barrier_semaphore()

    def greet(unit, x, s, p):
        pl.semaphore_signal(barrier, inc=1, device_id=(x, s), device_id_type=MESH)

    all_partners(True, greet)

    dest = dest_ref[...]
    onehot = (dest == iota((DEVICES, TILES), 0)).astype(F32)
    before = (iota((TILES, TILES), 0) < iota((TILES, TILES), 1)).astype(BF16)
    rank = jnp.sum(dot(onehot.astype(BF16), before) * onehot, axis=0, keepdims=True)
    slots = dest.astype(F32) * CAP + rank
    slot_col[...] = jnp.transpose(jnp.broadcast_to(slots, (128, TILES)))
    slot_row = slots.astype(jnp.int32)

    loads[0].wait()
    loads[1].wait()
    for i in range(4):
        rows = pl.ds(i * 128, 128)
        tile_rows = dot(feats[rows, :], embed_w[...]).astype(BF16)
        embedded[rows, :] = tile_rows
        normed[rows, :] = layer_norm(tile_rows.astype(F32), gain1_ref[...].reshape(1, D))

    def pack(i, carry):
        chosen = (iota((256, TILES), 0) + i * 256 == slot_row).astype(F32)
        rows = dot(chosen.astype(BF16), normed[...])
        used = jnp.sum(chosen, axis=1, keepdims=True)
        first = jnp.where((iota((256, 128), 1) == 0) & (used < 0.5), EMPTY, rows[:, :128])
        send1[pl.ds(i * 32, 32)] = to_message(jnp.concatenate([first, rows[:, 128:]], axis=1))
        return carry

    lax.fori_loop(0, 4, pack, 0)
    pl.semaphore_wait(barrier, DEVICES - 1)

    def send_rows(unit, x, s, p):
        pltpu.make_async_remote_copy(
            src_ref=send1.at[x * N_SEQ + s], dst_ref=recv1.at[unit * 8 + place], send_sem=send1_sem,
            recv_sem=recv1_sem.at[unit // 4], device_id=(x, s), device_id_type=MESH,
        ).start()

    all_partners(True, send_rows)
    pltpu.make_async_copy(send1.at[me], recv1.at[12 * 8 + place], recv1_sem.at[3]).start()

    loads[2].wait()

    def turn(i, carry):
        columns = pl.ds(pl.multiple_of(i * 128, 128), 128)
        qkv_t[columns, :] = jnp.transpose(qkv_w[:, columns].astype(F32)).astype(BF16)
        return carry

    lax.fori_loop(0, 3 * D // 128, turn, 0)
    one_row = (iota((16, SLOTS), 0) == 0).astype(BF16)
    for h in range(HEADS):
        base = 64 * (h % 2)
        q_t[h, pl.ds(64 - base, 64), :] = jnp.zeros((64, SLOTS), BF16)
        q_t[h, pl.ds(base + HEAD, 16), :] = one_row
        v_t[h, pl.ds(HEAD, 16), :] = jnp.ones((16, SLOTS), BF16)

    def project(g, carry):
        group = recv1.at[pl.ds(g * 32, 32)]
        pltpu.make_async_copy(group, group, recv1_sem.at[g]).wait()
        rows = from_message(recv1[pl.ds(g * 32, 32)])
        empty = rows[:, 0:1] > 0.1 * EMPTY
        rows = jnp.where(empty, 0.0, rows).astype(BF16)
        bias = jnp.broadcast_to(jnp.where(empty, MASKED, 0.0), (256, 128))
        lanes = pl.ds(pl.multiple_of(g * 256, 256), 256)
        query = (lax.dot_general(qkv_t[0:D, :], rows, NT, preferred_element_type=F32) * SCALE).astype(BF16)
        for h in range(HEADS):
            q_t[h, pl.ds(64 * (h % 2), HEAD), lanes] = query[h * HEAD : (h + 1) * HEAD]
        key = lax.dot_general(qkv_t[D : 2 * D, :], rows, NT, preferred_element_type=F32)
        masks = jnp.where(iota((16, 256), 0) == 0, jnp.transpose(bias)[0:16, :], 0.0)
        for p in range(HEADS // 2):
            pair = jnp.concatenate(
                [key[96 * p : 96 * p + 48], masks, key[96 * p + 48 : 96 * p + 96], masks], axis=0
            )
            k_ref[p, pl.ds(pl.multiple_of(g * 256, 256), 256), :] = jnp.transpose(pair).astype(BF16)
        value = lax.dot_general(qkv_t[2 * D :, :], rows, NT, preferred_element_type=F32).astype(BF16)
        for h in range(HEADS):
            v_t[h, pl.ds(0, HEAD), lanes] = value[h * HEAD : (h + 1) * HEAD]
        lane, column = iota((256, 256), 0), iota((256, 256), 1)
        taken = ((lane & (RATE - 1)) == (column >> 4)) & (g * 4 + (lane >> 6) == unit_of(column & 15))
        taken = taken.astype(BF16)
        owner = iota((HEAD, 256), 1) >> 4
        for n, part in enumerate((query, key.astype(BF16), value)):
            wide = dot(part, taken)
            own = jnp.zeros((HEAD, 256), F32)
            for h in range(HEADS):
                own = own + jnp.where(owner == h, wide[h * HEAD : (h + 1) * HEAD], 0.0)
            far_cols[n * HEAD : (n + 1) * HEAD, :] += own
        far_cols[3 * HEAD :, :] += dot(masks.astype(BF16), taken)
        return carry

    far_cols[...] = jnp.zeros_like(far_cols)
    lax.fori_loop(0, 4, project, 0)

    one = jnp.where(iota((16, 256), 0) == 0, 1.0, 0.0)
    far_q = jnp.concatenate([far_cols[0:HEAD, :], one, jnp.zeros((64, 256), F32)], axis=0)
    far_kv = jnp.concatenate(
        [far_cols[HEAD : 2 * HEAD, :], far_cols[3 * HEAD :, :], far_cols[2 * HEAD : 3 * HEAD, :], one], axis=0
    )
    far_send[...] = jnp.concatenate(
        [jnp.transpose(far_q).reshape(HEADS, ROWS, 128), jnp.transpose(far_kv).reshape(HEADS, ROWS, 128)], axis=1
    ).astype(BF16)

    mine = sq // 2

    def send_far(h, s):
        pltpu.make_async_remote_copy(
            src_ref=far_send.at[h], dst_ref=far_recv.at[sq], send_sem=fsend_sem, recv_sem=frecv_sem,
            device_id=(dp, s), device_id_type=MESH,
        ).start()

    for i in range(1, HEADS):
        h = lax.rem(mine + i, HEADS)
        send_far(h, 2 * h)
        send_far(h, 2 * h + 1)
    send_far(mine, 2 * mine + 1 - c0)
    pltpu.make_async_copy(far_send.at[mine], far_recv.at[sq], frecv_sem).start()

    parts = SLOTS // QUERIES

    def score(h, i):
        return lax.dot_general(
            k_ref[h // 2], q_t[h, :, i * QUERIES : (i + 1) * QUERIES], (((1,), (0,)), ((), ())), preferred_element_type=F32
        )

    def attend_head(h, act=None):
        for i in range(parts):
            if i + 1 < parts:
                later = score(h, i + 1)
            else:
                later = score(jnp.minimum(h + 1, HEADS - 1) if not isinstance(h, int) else min(h + 1, HEADS - 1), 0)
            if act is not None and i == 0:
                act()
            block = scores[i % 2]
            top = jnp.max(block, axis=0, keepdims=True)
            weights = jnp.exp2(block - top).astype(BF16)
            near[h, :, i * QUERIES : (i + 1) * QUERIES] = dot(v_t[h], weights)
            peak[h, :, i * QUERIES : (i + 1) * QUERIES] = jnp.broadcast_to(top, (8, QUERIES))
            scores[(i + 1) % 2] = later

    def attend(first, last):
        for h in range(first, last):
            attend_head(h)

    def attend_and_send(first, c):
        def one_head(t, carry):
            attend_head(first + t, lambda: each_partner(t, False, send_back(c), False))
            return carry

        lax.fori_loop(0, 3, one_head, 0)
        attend_head(first + 3, lambda: each_partner(3, False, send_back(c), True))
        attend_head(first + 4)

    def far_branch():
        pltpu.make_async_copy(far_recv, far_recv, frecv_sem).wait()
        half = N_SEQ // 2
        queries = far_recv[pl.ds(half * c0, half), pl.ds(0, 16), :].reshape(half * ROWS, 128)
        pairs = far_recv[:, pl.ds(16, 16), :].reshape(N_SEQ * ROWS, 128)
        block = lax.dot_general(queries, pairs, NT, preferred_element_type=F32)
        top = jnp.max(block, axis=1, keepdims=True)
        result = dot(jnp.exp2(block - top).astype(BF16), pairs)
        summed = result[:, 64 + HEAD : 65 + HEAD]
        result = jnp.where(iota(result.shape, 1) < 64, top + jnp.log2(summed), result / summed)
        res_send[...] = result.reshape(half, ROWS, 128)

        def answer(i):
            to = lax.rem(sq + i, half)
            pltpu.make_async_remote_copy(
                src_ref=res_send.at[to], dst_ref=res_recv.at[mine], send_sem=rsend_sem, recv_sem=rrecv_sem,
                device_id=(dp, half * c0 + to), device_id_type=MESH,
            ).start()

        for i in range(1, half):
            answer(i)

        @pl.when(sq // half != c0)
        def _():
            answer(0)

        @pl.when(sq // half == c0)
        def _():
            pltpu.make_async_copy(res_send.at[lax.rem(sq, half)], res_recv.at[mine], rrecv_sem).start()

    def far_arrived():
        pltpu.make_async_copy(res_recv, res_recv, rrecv_sem).wait()
        results = res_recv[...].reshape(HEADS * ROWS, 128)
        results_ref[...] = res_recv[...]
        lane = iota((HEADS * ROWS, 128), 1)
        high = results.astype(BF16).astype(F32)
        middle = (results - high).astype(BF16).astype(F32)
        lowest = results - high - middle
        split = jnp.where(lane >= 64, results, jnp.where(lane == 0, high, jnp.where(lane == 1, middle, lowest)))
        row = iota((HEADS * ROWS, SLOTS), 0)
        spread = (iota((HEADS * ROWS, SLOTS), 1) == unit_of(row & 15) * RATE + (row >> 4)).astype(BF16)
        far_t[...] = lax.dot_general(split.astype(BF16), spread, TN, preferred_element_type=F32)

    def blend(first, last):
        def one_head(h, carry):
            summed = near[h, HEAD : HEAD + 1, :]
            near_lse = peak[h, 0:1, :] + jnp.log2(summed)
            far_lse = far_t[0:1, :] + far_t[1:2, :] + far_t[2:3, :]
            far_lse = jnp.where((iota((1, SLOTS), 1) & (RATE - 1)) == h, far_lse, MASKED)
            larger = jnp.maximum(near_lse, far_lse)
            near_weight = jnp.exp2(near_lse - larger)
            far_weight = jnp.exp2(far_lse - larger)
            both = near_weight + far_weight
            joined = near[h, 0:HEAD, :] * (near_weight / (both * summed)) + far_t[64 : 64 + HEAD, :] * (far_weight / both)
            mixed[pl.ds(pl.multiple_of(h * HEAD, 16), HEAD), :] = joined.astype(BF16)
            return carry

        lax.fori_loop(first, last, one_head, 0)

    def pack_back(c):
        def some(g, carry):
            lanes = pl.ds(pl.multiple_of(g * 256, 256), 256)
            rows = jnp.transpose(mixed[256 * c : 256 * (c + 1), lanes].astype(F32))
            send2[c, pl.ds(g * 32, 32)] = to_message(rows)
            return carry

        lax.fori_loop(0, 4, some, 0)
        pltpu.make_async_copy(send2.at[c, 12 * 8 + place], recv2.at[c, me], keep_sem.at[c]).start()

    def send_back(c):
        def act(unit, x, s, p):
            pltpu.make_async_remote_copy(
                src_ref=send2.at[c, unit * 8 + p], dst_ref=recv2.at[c, me], send_sem=send2_sem.at[c],
                recv_sem=recv2_sem.at[c], device_id=(x, s), device_id_type=MESH,
            ).start()

        return act

    scores[0] = score(0, 0)
    attend(0, 3)
    far_branch()
    attend(3, 6)
    far_arrived()
    blend(0, 6)
    pack_back(0)
    attend_and_send(6, 0)
    blend(6, 11)
    pack_back(1)
    attend_and_send(11, 1)
    blend(11, 16)
    pack_back(2)
    all_partners(False, send_back(2))

    loads[3].wait()
    hidden[...] = embedded[...].astype(F32)
    for c in range(3):
        pltpu.make_async_copy(send2.at[c, 12 * 8 + place], recv2.at[c, me], keep_sem.at[c]).wait()
        most = recv2.at[c, pl.ds(0, DEVICES - 1)]
        pltpu.make_async_copy(most, most, recv2_sem.at[c]).wait()
        taken = jnp.zeros((TILES, 256), F32)
        for g in range(4):
            chosen = (iota((TILES, 256), 1) + g * 256 == slot_col[:, 0:1].astype(jnp.int32)).astype(BF16)
            taken = taken + dot(chosen, from_message(recv2[c, pl.ds(g * 32, 32)]).astype(BF16))
        hidden[...] += dot(taken.astype(BF16), out_w[256 * c : 256 * (c + 1), :])
    state_ref[...] = hidden[...].astype(BF16)

    most = pl.ds(0, DEVICES - 1)
    pltpu.make_async_copy(send1.at[most], send1.at[most], send1_sem).wait()
    for c in range(3):
        pltpu.make_async_copy(send2.at[c, most], send2.at[c, most], send2_sem.at[c]).wait()

    most = far_recv.at[pl.ds(0, N_SEQ - 1)]
    pltpu.make_async_copy(most, most, fsend_sem).wait()

    @pl.when(sq // 16 == c0)
    def _():
        most = res_send.at[pl.ds(0, 15)]
        pltpu.make_async_copy(most, most, rsend_sem).wait()

    @pl.when(sq // 16 != c0)
    def _():
        pltpu.make_async_copy(res_send, res_send, rsend_sem).wait()


def feed_kernel(
    state_ref, results_ref, gain2_ref, up_hbm, down_hbm, tile_ref, far_ref, up_w, down_w, normed, total, scores, load_sem
):
    def load(i):
        part = pl.ds(i * FF_BLOCK if isinstance(i, int) else pl.multiple_of(i * FF_BLOCK, FF_BLOCK), FF_BLOCK)
        return (
            pltpu.make_async_copy(up_hbm.at[:, part], up_w.at[:, part], load_sem.at[0, i]),
            pltpu.make_async_copy(down_hbm.at[part, :], down_w.at[part, :], load_sem.at[1, i]),
        )

    def arrive(i):
        for copy in load(i):
            copy.wait()

    for i in range(FF // FF_BLOCK):
        for copy in load(i):
            copy.start()
    far_ref[...] = results_ref[:, :, 64 : 64 + HEAD]
    state = state_ref[...].astype(F32)
    normed[...] = layer_norm(state, gain2_ref[...].reshape(1, D))
    total[...] = state

    def columns(i):
        return pl.ds(i * FF_BLOCK if isinstance(i, int) else pl.multiple_of(i * FF_BLOCK, FF_BLOCK), FF_BLOCK)

    def feed(i, slot, last):
        if not last:
            arrive(i + 1)
            later = dot(normed[...], up_w[:, columns(i + 1)])
        inner = jax.nn.gelu(scores[slot], approximate=True).astype(BF16)
        total[...] += dot(inner, down_w[columns(i), :])
        if not last:
            scores[1 - slot] = later

    def feed_two(k, carry):
        feed(2 * k, 0, False)
        feed(2 * k + 1, 1, False)
        return carry

    arrive(0)
    scores[0] = dot(normed[...], up_w[:, columns(0)])
    lax.fori_loop(0, FF // FF_BLOCK // 2 - 1, feed_two, 0)
    feed(FF // FF_BLOCK - 2, 0, False)
    feed(FF // FF_BLOCK - 1, 1, True)
    tile_ref[...] = total[...].astype(BF16)


def on_device(tile_feats, tile_dest, embed_weight, norm1_gain, qkv_weight, out_weight, norm2_gain, up_weight, down_weight):
    hbm = pl.BlockSpec(memory_space=pl.ANY)
    vmem = pl.BlockSpec(memory_space=pltpu.VMEM)
    dma = pltpu.SemaphoreType.DMA
    state, results = pl.pallas_call(
        kernel,
        out_shape=(
            jax.ShapeDtypeStruct((TILES, D), BF16),
            jax.ShapeDtypeStruct((HEADS, ROWS, 128), F32),
        ),
        in_specs=[hbm, vmem, hbm, vmem, hbm, hbm],
        out_specs=(vmem, vmem),
        scratch_shapes=[
            pltpu.VMEM((TILES, F), BF16),
            pltpu.VMEM((F, D), BF16),
            pltpu.VMEM((D, 3 * D), BF16),
            pltpu.VMEM((D, D), BF16),
            pltpu.VMEM((3 * D, D), BF16),
            pltpu.VMEM((TILES, D), BF16),
            pltpu.VMEM((TILES, D), BF16),
            pltpu.VMEM((TILES, 128), F32),
            pltpu.VMEM((DEVICES, 16, 384), BF16),
            pltpu.VMEM((DEVICES, 16, 384), BF16),
            pltpu.VMEM((HEADS, 128, SLOTS), BF16),
            pltpu.VMEM((HEADS // 2, SLOTS, 128), BF16),
            pltpu.VMEM((HEADS, 64, SLOTS), BF16),
            pltpu.VMEM((2, SLOTS, QUERIES), F32),
            pltpu.VMEM((HEADS, 64, SLOTS), F32),
            pltpu.VMEM((HEADS, 8, SLOTS), F32),
            pltpu.VMEM((D, SLOTS), BF16),
            pltpu.VMEM((3 * HEAD + 16, 256), F32),
            pltpu.VMEM((HEADS, 32, 128), BF16),
            pltpu.VMEM((N_SEQ, 32, 128), BF16),
            pltpu.VMEM((N_SEQ // 2, ROWS, 128), F32),
            pltpu.VMEM((HEADS, ROWS, 128), F32),
            pltpu.VMEM((128, SLOTS), F32),
            pltpu.VMEM((3, DEVICES, 16, 128), BF16),
            pltpu.VMEM((3, DEVICES, 16, 128), BF16),
            pltpu.VMEM((TILES, D), F32),
            dma((4,)),
            dma,
            dma((4,)),
            dma,
            dma,
            dma,
            dma,
            dma((3,)),
            dma((3,)),
            dma((3,)),
        ],
        compiler_params=pltpu.CompilerParams(collective_id=0, has_side_effects=True, vmem_limit_bytes=62 << 20),
    )(
        tile_feats, tile_dest.reshape(1, TILES), embed_weight, norm1_gain, qkv_weight, out_weight
    )
    tile_out, far_heads = pl.pallas_call(
        feed_kernel,
        out_shape=(
            jax.ShapeDtypeStruct((TILES, D), BF16),
            jax.ShapeDtypeStruct((HEADS, ROWS, HEAD), F32),
        ),
        in_specs=[vmem, vmem, vmem, hbm, hbm],
        out_specs=(vmem, vmem),
        scratch_shapes=[
            pltpu.VMEM((D, FF), BF16),
            pltpu.VMEM((FF, D), BF16),
            pltpu.VMEM((TILES, D), BF16),
            pltpu.VMEM((TILES, D), F32),
            pltpu.VMEM((2, TILES, FF_BLOCK), F32),
            dma((2, FF // FF_BLOCK)),
        ],
        compiler_params=pltpu.CompilerParams(vmem_limit_bytes=50 << 20),
    )(state, results, norm2_gain, up_weight, down_weight)
    return tile_out, far_heads[None]


def solution(mesh):
    return jax.shard_map(
        on_device,
        mesh=mesh,
        in_specs=(P(("dp", "seq"), None), P(("dp", "seq"), None), P(), P(), P(), P(), P(), P(), P()),
        out_specs=(P(("dp", "seq"), None), P("dp", None, "seq", None)),
        check_vma=False,
    )
```
